256 devices in a mesh: var: 32 (over z, y_hi, core), tp: 8 (over x, y_lo).
Axes of the slice: x: 4, y: 4 (y_hi: 2, y_lo: 2; y = y_hi * 2 + y_lo), z: 8, core: 2. Of those that a mesh axis runs over, the one named last changes fastest.
Arguments:
- patches: bfloat16 [128, 64, 4096], P('var', None, 'tp'), may hold values from -6 to 6
- slot_weight: bfloat16 [128, 64, 1024], P('var'), may hold values from -0.75 to 0.75
- slot_bias: float32 [128, 1024], P('var'), may hold values from -3 to 3
- var_embed: float32 [91, 1024], replicated, may hold values from -3 to 3
- owner_count: int32 [32], P('var'), may hold values from 1 to 4, as said below
- slot_variable: int32 [128], P('var'), may hold values from 0 to 90, as said below
- key_query: bfloat16 [1024, 16], replicated, may hold values from -20 to 20
- value_weight: bfloat16 [1024, 1024], replicated, may hold values from -0.1875 to 0.1875
- norm_gain: float32 [1024], replicated, may hold values from 0.25 to 1.75
- qkv_weight: bfloat16 [1024, 3, 1024], P(None, None, 'tp'), may hold values from -4 to 4
- token_grad: float32 [4096, 1024], P(('var', 'tp')), may hold values from -0.09375 to 0.09375
Outputs:
- layer_out: float32 [4096, 1024], P('var', 'tp')
- embed_grad: float32 [128, 64, 1024], P('var', None, 'tp')
The draws below stay inside these ranges and needn't reach their ends.
Inputs may be any that keep to these rules, and one draw needn't show every extreme that they name: `owner_count`: the counts of all owners add up to 91; some owner has 4. `slot_variable`: the live slots (those below their owner's count) name each variable exactly once; the other slots hold any variable number.
All inputs are finite; a program needn't handle non-finite values.
Results may differ from the reference program's by a relative error of at most 0.04.
The reference program's roundings to bfloat16 on the way (of `embedded`, `aggregated`, `tokens`, `normed`, `projected`, `dscore`, `dvalue` and `dembed`) count: a program that leaves them out, or rounds other values in their place, can miss the bound.
Values may be sent and summed in bfloat16 or wider, within the bound.
A program may use at most 192 MiB of HBM per device.

```python
import jax
import jax.numpy as jnp
from jax import lax

D = 1024
HEADS = 16
VARS = 91
PATCH = 64
VSLOT = 4
SLOTS = 128
TOKENS = 4096
TOK_TP = 512
PIECE = 16
N_VAR = 32
N_TP = 8


def owner_tables(key):
    owner_order = jax.random.permutation(jax.random.fold_in(key, 11), N_VAR)
    owner_rank = jnp.argsort(owner_order).astype(jnp.int32)
    extra_slots = jnp.clip(VARS - N_VAR - (VSLOT - 1) * owner_rank, 0, VSLOT - 1)
    counts = (1 + extra_slots).astype(jnp.int32)
    starts = jnp.cumsum(counts) - counts
    variables = jax.random.permutation(jax.random.fold_in(key, 12), VARS).astype(jnp.int32)
    slot_ids = jnp.arange(SLOTS, dtype=jnp.int32)
    owner_ids = slot_ids // VSLOT
    local_ids = slot_ids % VSLOT
    live_slot = local_ids < counts[owner_ids]
    position = jnp.clip(starts[owner_ids] + local_ids, 0, VARS - 1)
    filler = jax.random.randint(jax.random.fold_in(key, 13), (SLOTS,), 0, VARS, dtype=jnp.int32)
    return (counts, jnp.where(live_slot, variables[position], filler).astype(jnp.int32))


def draw_owner_count(key, part):
    counts, table = owner_tables(key)
    return counts


def draw_slot_variable(key, part):
    counts, table = owner_tables(key)
    return table


def draw_key_query(key, part):
    key = jax.random.fold_in(key, 3)
    sample = jnp.clip(jax.random.normal(key, (D, HEADS), jnp.float32), -5.0, 5.0) * D ** (-0.5)
    return (sample * 2.0).astype(jnp.bfloat16)


def draw_qkv_weight(key, part):
    key = jax.random.fold_in(key, 5)
    sample = jnp.clip(jax.random.normal(key, (D, 3, D), jnp.float32), -5.0, 5.0) * D ** (-0.5)
    return sample.astype(jnp.bfloat16)


def level_of(key, dims, pieces, least, high):
    level, own = 1.0, jax.random.fold_in(key, 6)
    for axis_at, blocks in pieces:
        heights = jnp.exp(jax.random.uniform(jax.random.fold_in(own, axis_at), (blocks,), jnp.float32, least / len(pieces), high / len(pieces)))
        level = level * jnp.repeat(heights, dims[axis_at] // blocks).reshape([-1 if axis == axis_at else 1 for axis in range(len(dims))])
    return level


def gaussian(key, shape, deviation, bound, split=(), held_as=jnp.bfloat16):
    values = deviation * jax.random.normal(key, shape, jnp.float32)
    if split:
        values = values * level_of(key, shape, split, -0.22, 0.18)
    return jnp.clip(values, -bound, bound).astype(held_as)


def setup_inputs(seed: int = 0) -> dict:
    arg_keys = jax.random.split(jax.random.key(seed), 12)
    return {
        "patches": gaussian(arg_keys[0], (SLOTS, PATCH, TOKENS), 1.0, 6.0, ((0, 32), (2, 8))),
        "slot_weight": gaussian(arg_keys[1], (SLOTS, PATCH, D), PATCH ** -0.5, 0.75, ((0, 32),)),
        "slot_bias": gaussian(arg_keys[2], (SLOTS, D), 0.5, 3.0, ((0, 32),), jnp.float32),
        "var_embed": gaussian(arg_keys[3], (VARS, D), 0.5, 3.0, (), jnp.float32),
        "owner_count": draw_owner_count(jax.random.fold_in(arg_keys[11], 71), 0),
        "slot_variable": draw_slot_variable(jax.random.fold_in(arg_keys[11], 71), 0),
        "key_query": draw_key_query(jax.random.fold_in(arg_keys[11], 71), 0),
        "value_weight": gaussian(arg_keys[7], (D, D), D ** -0.5, 0.1875),
        "norm_gain": jnp.clip(1.0 + 0.15 * jax.random.normal(arg_keys[8], (D,), jnp.float32), 0.25, 1.75),
        "qkv_weight": draw_qkv_weight(jax.random.fold_in(arg_keys[11], 71), 0),
        "token_grad": gaussian(arg_keys[10], (TOKENS, D), (TOKENS ** -0.5), 0.09375, ((0, 256),), jnp.float32),
    }


def spread_heads(values, head_dim):
    return jnp.repeat(values, head_dim, axis=-1)

def head_sums(values, head_count):
    return lax.optimization_barrier(jnp.sum(values.reshape(values.shape[:-1] + (head_count, values.shape[-1] // head_count)), axis=-1))

def reference(patches, slot_weight, slot_bias, var_embed, owner_count, slot_variable, key_query, value_weight, norm_gain, qkv_weight, token_grad):
    head_dim = D // HEADS
    slot_ids = jnp.arange(SLOTS).astype(jnp.int32)
    live_slot = slot_ids % VSLOT < owner_count[slot_ids // VSLOT]
    offsets = slot_bias + var_embed[slot_variable]
    grad_tok = token_grad.reshape(N_VAR, N_TP, PIECE, D).transpose(1, 0, 2, 3).reshape(TOKENS, D)

    def span_step(grad_total, column):
        first_tok = (column * TOK_TP).astype(jnp.int32)
        patch_block = lax.dynamic_slice_in_dim(patches, first_tok, TOK_TP, 2).astype(jnp.float32)
        grad_block = lax.dynamic_slice_in_dim(grad_tok, first_tok, TOK_TP, 0)
        embedded = (jnp.einsum('spt,spd->std', patch_block, slot_weight.astype(jnp.float32)) + offsets[:, None, :]).astype(jnp.bfloat16)
        embedded_f = embedded.astype(jnp.float32)
        scores = jnp.einsum('std,dh->sth', embedded_f, key_query.astype(jnp.float32))
        scores = jnp.where(live_slot[:, None, None], scores, -jnp.inf)
        slot_values = jnp.einsum('std,de->ste', embedded_f, value_weight.astype(jnp.float32))
        row_top = lax.optimization_barrier(jnp.max(scores, axis=0))
        raw_weights = jnp.exp(scores - row_top[None])
        slot_probs = raw_weights / lax.optimization_barrier(jnp.sum(raw_weights, axis=0))[None]
        aggregated = lax.optimization_barrier(jnp.sum(spread_heads(slot_probs, head_dim) * slot_values, axis=0)).astype(jnp.bfloat16)
        token_inner = head_sums(grad_block * aggregated.astype(jnp.float32), HEADS)
        slot_inner = head_sums(slot_values * grad_block[None], HEADS)
        dscore = (slot_probs * (slot_inner - token_inner[None])).astype(jnp.bfloat16)
        dvalue = (spread_heads(slot_probs, head_dim) * grad_block[None]).astype(jnp.bfloat16)
        dembed = (jnp.einsum('ste,de->std', dvalue.astype(jnp.float32), value_weight.astype(jnp.float32)) + jnp.einsum('sth,dh->std', dscore.astype(jnp.float32), key_query.astype(jnp.float32))).astype(jnp.bfloat16)
        grad_term = jnp.einsum('spt,std->spd', patch_block, dembed.astype(jnp.float32))
        return (grad_total + grad_term, aggregated)
    grad_total, agg_spans = lax.scan(span_step, jnp.zeros((SLOTS, PATCH, D), jnp.float32), jnp.arange(N_TP).astype(jnp.int32))
    tokens = agg_spans.reshape(N_TP, N_VAR, PIECE, D).transpose(1, 0, 2, 3).reshape(TOKENS, D)
    tokens_f = tokens.astype(jnp.float32)
    row_mean = lax.optimization_barrier(jnp.mean(tokens_f, axis=1, keepdims=True))
    centred = tokens_f - row_mean
    row_var = lax.optimization_barrier(jnp.mean(centred * centred, axis=1, keepdims=True))
    normed = (centred * lax.rsqrt(row_var + 1e-05) * norm_gain).astype(jnp.bfloat16)
    projected = jnp.einsum('td,dke->tke', normed.astype(jnp.float32), qkv_weight.astype(jnp.float32)).astype(jnp.bfloat16)
    score_scale = head_dim ** (-0.5)

    def head_step(head_index):
        first_col = (head_index * head_dim).astype(jnp.int32)
        query_head = lax.dynamic_slice_in_dim(projected[:, 0, :], first_col, head_dim, 1)
        key_head = lax.dynamic_slice_in_dim(projected[:, 1, :], first_col, head_dim, 1)
        val_head = lax.dynamic_slice_in_dim(projected[:, 2, :], first_col, head_dim, 1)
        logits = jnp.dot(query_head, key_head.T, preferred_element_type=jnp.float32) * score_scale
        row_top = lax.optimization_barrier(jnp.max(logits, axis=1, keepdims=True))
        kernel = jnp.exp(logits - row_top)
        row_total = lax.optimization_barrier(jnp.sum(kernel, axis=1, keepdims=True))
        return jnp.dot(kernel.astype(jnp.bfloat16), val_head, preferred_element_type=jnp.float32) / row_total
    head_outputs = lax.map(head_step, jnp.arange(HEADS).astype(jnp.int32))
    mixed_heads = head_outputs.transpose(1, 0, 2).reshape(TOKENS, D)
    layer_out = tokens_f + mixed_heads
    return (layer_out, grad_total)
```

```python
import functools

import jax
import jax.numpy as jnp
from jax import lax
from jax.experimental import pallas as pl
from jax.experimental.pallas import tpu as pltpu
from jax.sharding import PartitionSpec as P

F32 = jnp.float32
BF16 = jnp.bfloat16
MESH = pl.DeviceIdType.MESH
LANES = 128
NEG = float("-inf")
GRAD_T = F32
NZ, NY, NC = 8, 2, 2
NX, NL = 4, 2


def iota(shape, axis):
    return lax.broadcasted_iota(jnp.int32, shape, axis)


def near(k):
    return jnp.where(lax.rem(k, 2) == 1, (k + 1) // 2, lax.rem(NZ - k // 2, NZ))


def far(k):
    return jnp.where(lax.rem(k, 2) == 0, NZ // 2 + k // 2, NZ // 2 - 1 - k // 2)


def dot(a, b):
    return jnp.dot(a, b, preferred_element_type=F32)


def dot_nt(a, b):
    return lax.dot_general(a, b, (((1,), (1,)), ((), ())), preferred_element_type=F32)


def dot_tn(a, b):
    return lax.dot_general(a, b, (((0,), (0,)), ((), ())), preferred_element_type=F32)


def lane(rows):
    return iota((rows, LANES), 1)


def unpack_two(x):
    left = lane(x.shape[0]) < 64
    turned = pltpu.roll(x, 64, 1)
    return jnp.where(left, x, turned), jnp.where(left, turned, x)


def head_total(x):
    total = x[:, 0:LANES]
    for i in range(1, x.shape[1] // LANES):
        total = total + x[:, i * LANES : (i + 1) * LANES]
    for shift in (64, 32, 16):
        total = total + pltpu.roll(total, shift, 1)
    return total


def wide(x, width):
    return jnp.concatenate([x] * (width // LANES), axis=1)


def merged(first, second, width):
    m1, l1 = unpack_two(first[:, width:])
    m2, l2 = unpack_two(second[:, width:])
    top = jnp.maximum(m1, m2)
    e1, e2 = jnp.exp(m1 - top), jnp.exp(m2 - top)
    total = l1 * e1 + l2 * e2
    sums = first[:, :width] * wide(e1, width) + second[:, :width] * wide(e2, width)
    return sums, top, total


def packed_two(top, total):
    return jnp.where(lane(top.shape[0]) < 64, top, total)


def kernel(
    patches,
    slot_weight,
    slot_bias,
    var_embed,
    owner_count,
    slot_variable,
    key_query,
    value_weight,
    norm_gain,
    qkv_weight,
    token_grad,
    layer_out,
    embed_grad,
    perm,
    wvp,
    kq_rep,
    emb,
    values,
    scores,
    raw,
    part,
    sib_in,
    y_out,
    y_in,
    z_out,
    z_in,
    grads,
    stats,
    tops,
    invs,
    inners,
    tokens,
    queries,
    kv,
    run_top,
    run_sum,
    run_acc,
    dvalue,
    dembed,
    gterm,
    x_in,
    l_out,
    l_in,
    bs,
    br,
    gs,
    gr,
    ts,
    tr,
    rs,
    rr,
):
    slots, pixels, rows = patches.shape
    width = value_weight.shape[0]
    heads = key_query.shape[1]
    piece = token_grad.shape[0]
    head_dim = width // heads
    seq = tokens.shape[0] * piece
    cols = layer_out.shape[1]
    zrows = rows // NZ

    v, j = lax.axis_index("var"), lax.axis_index("tp")
    z, y, c = v // 4, lax.rem(v // 2, 2), lax.rem(v, 2)
    x, w = j // 2, lax.rem(j, 2)

    def at_z(dz):
        return {"var": lax.rem(z + dz, NZ) * 4 + y * 2 + c, "tp": j}

    y_mate = {"var": z * 4 + (1 - y) * 2 + c, "tp": j}
    c_mate = {"var": z * 4 + y * 2 + (1 - c), "tp": j}
    l_mate = {"var": v, "tp": x * 2 + (1 - w)}

    def at_tp(d):
        return {"var": v, "tp": lax.rem(j + d, NX * NL)}

    def at_x(d):
        return {"var": v, "tp": lax.rem(x + d, NX) * 2 + w}

    def send(src, dst, ssem, rsem, device):
        return pltpu.make_async_remote_copy(
            src_ref=src, dst_ref=dst, send_sem=ssem, recv_sem=rsem, device_id=device, device_id_type=MESH
        )

    barrier = pltpu.get_barrier_semaphore()

    def greet_z(d, carry):
        pl.semaphore_signal(barrier, inc=1, device_id=at_z(d), device_id_type=MESH)
        return carry

    def greet_tp(d, carry):
        pl.semaphore_signal(barrier, inc=1, device_id=at_tp(d), device_id_type=MESH)
        return carry

    lax.fori_loop(1, NZ, greet_z, 0)
    lax.fori_loop(1, NX * NL, greet_tp, 0)
    pl.semaphore_signal(barrier, inc=1, device_id=y_mate, device_id_type=MESH)
    pl.semaphore_signal(barrier, inc=1, device_id=c_mate, device_id_type=MESH)

    def g_z(buf, n, k):
        zk = lax.rem(z - near(k) + NZ, NZ)
        here = buf.at[zk, y, c]
        return send(here, here, gs.at[n, k], gr.at[n, k], at_z(near(k)))

    def g_start(buf, n):
        def one(k, carry):
            own = buf.at[z, y, c]
            send(own, own, gs.at[n, k], gr.at[n, k], at_z(near(k))).start()
            return carry

        lax.fori_loop(1, NZ, one, 0)

    def g_y(buf, n, k):
        zk = lax.rem(z - near(k) + NZ, NZ)
        here = buf.at[zk, y, c]
        return send(here, here, gs.at[n, NZ + k], gr.at[n, NZ + k], y_mate)

    def g_c(buf, n, k):
        zk = lax.rem(z - near(k) + NZ, NZ)
        here = buf.at[zk, pl.ds(0, NY), c]
        return send(here, here, gs.at[n, 2 * NZ + k], gr.at[n, 2 * NZ + k], c_mate)

    def g_pass_y(buf, n, k):
        @pl.when(k > 0)
        def _():
            g_z(buf, n, k).wait_recv()

        g_y(buf, n, k).start()

    def g_pass_c(buf, n, k):
        g_y(buf, n, k).wait_recv()
        g_c(buf, n, k).start()

    def g_take(buf, n, k):
        g_c(buf, n, k).wait_recv()

    def g_drain(buf, n):
        def one(k, carry):
            @pl.when(k > 0)
            def _():
                g_z(buf, n, k).wait_send()

            g_y(buf, n, k).wait_send()
            g_c(buf, n, k).wait_send()
            return carry

        lax.fori_loop(0, NZ, one, 0)

    def make_perm(i, carry):
        cb = pl.multiple_of(i * 256, 256)
        row, col = iota((width, 256), 0), iota((width, 256), 1) + cb
        hit = lax.rem(row, head_dim) * heads + row // head_dim == col
        block = jnp.where(hit, 1.0, 0.0).astype(BF16)
        perm[:, pl.ds(cb, 256)] = block
        wvp[:, pl.ds(cb, 256)] = dot(value_weight[...], block).astype(BF16)
        return carry

    lax.fori_loop(0, width // 256, make_perm, 0)

    g = token_grad[...]
    g1 = g.astype(BF16)
    g2f = g - g1.astype(F32)
    g2 = g2f.astype(BF16)
    g3 = (g2f - g2.astype(F32)).astype(BF16)
    gp = dot(jnp.concatenate([g1, g2, g3], axis=0), perm[...])
    gp = gp[0:piece] + (gp[piece : 2 * piece] + gp[2 * piece :])
    grads[z, y, c] = gp.astype(GRAD_T)

    pl.semaphore_wait(barrier, NZ - 1 + NX * NL - 1 + 2)
    g_start(grads, 0)

    spread = jnp.where(lax.rem(iota((heads, LANES), 1), heads) == iota((heads, LANES), 0), 1.0, 0.0).astype(BF16)
    kq_rep[...] = dot(key_query[...], spread).astype(BF16)

    for s in range(slots):
        offset = slot_bias[s : s + 1, :] + var_embed[pl.ds(slot_variable[s], 1), :]
        emb[s] = (dot_tn(patches[s], slot_weight[s]) + offset).astype(BF16)
        bias = jnp.where(s < owner_count[0], 0.0, NEG)
        scores[s] = dot(emb[s], kq_rep[...]) + bias
    top = scores[0]
    for s in range(1, slots):
        top = jnp.maximum(top, scores[s])
    total = jnp.zeros_like(top)
    for s in range(slots):
        e = jnp.exp(scores[s] - top)
        raw[s] = e
        total = total + e
    tops[...] = top
    invs[...] = total

    def b_c(k):
        return send(part.at[k, pl.ds(0, NY), 1 - c], sib_in.at[k], bs.at[0, k], br.at[0, k], c_mate)

    def b_y(k):
        return send(y_out.at[k], y_in.at[k], bs.at[1, k], br.at[1, k], y_mate)

    def b_z(k):
        return send(z_out.at[k], z_in.at[k], bs.at[2, k], br.at[2, k], at_z(far(k)))

    def first_stage(k):
        start = pl.multiple_of(lax.rem(z + far(k), NZ) * zrows, zrows)
        e = emb[:, pl.ds(start, zrows), :].reshape(slots * zrows, width)
        val = dot(e, wvp[...]).reshape(slots, zrows, width)
        values[:, pl.ds(start, zrows), :] = val
        for i in range(width // LANES):
            at = slice(i * LANES, (i + 1) * LANES)
            acc = raw[0, pl.ds(start, zrows), :] * val[0, :, at]
            for s in range(1, slots):
                acc = acc + raw[s, pl.ds(start, zrows), :] * val[s, :, at]
            part[k, :, :, :, at] = acc.reshape(NY, NC, piece, LANES)
        both = packed_two(tops[pl.ds(start, zrows), :], invs[pl.ds(start, zrows), :])
        part[k, :, :, :, width:] = both.reshape(NY, NC, piece, LANES)
        b_c(k).start()

    def second_stage(k):
        b_c(k).wait_recv()
        for out, at in ((y_out, 1 - y), (z_out, y)):
            sums, m, l = merged(part[k, at, c], sib_in[k, at], width)
            out[k, :, 0:width] = sums
            out[k, :, width:] = packed_two(m, l)
        b_y(k).start()

    def third_stage(k):
        b_y(k).wait_recv()
        sums, m, l = merged(z_out[k], y_in[k], width)

        @pl.when(k < NZ - 1)
        def _():
            z_out[k, :, 0:width] = sums
            z_out[k, :, width:] = packed_two(m, l)
            b_z(k).start()

        @pl.when(k == NZ - 1)
        def _():
            z_in[k, :, 0:width] = sums
            z_in[k, :, width:] = packed_two(m, l)

    def step(i, carry):
        @pl.when(i < NZ)
        def _():
            first_stage(i)

        @pl.when((i >= 1) & (i < NZ + 1))
        def _():
            second_stage(i - 1)

        @pl.when(i >= 2)
        def _():
            third_stage(i - 2)

        return carry

    lax.fori_loop(0, NZ + 2, step, 0)

    def grads_y(k, carry):
        g_pass_y(grads, 0, k)
        return carry

    lax.fori_loop(0, NZ, grads_y, 0)

    def arrived(k, carry):
        b_z(k).wait_recv()
        return carry

    lax.fori_loop(0, NZ - 1, arrived, 0)

    tl = [unpack_two(z_in[k, :, width:]) for k in range(NZ)]
    top = functools.reduce(jnp.maximum, [m for m, _ in tl])
    es = [jnp.exp(m - top) for m, _ in tl]
    total = functools.reduce(jnp.add, [l * e for (_, l), e in zip(tl, es)])
    sums = functools.reduce(jnp.add, [z_in[k, :, 0:width] * wide(es[k], width) for k in range(NZ)])
    inv = 1.0 / total
    agg = (sums / wide(total, width)).astype(BF16)
    tokens[j] = dot_nt(agg, perm[...]).astype(BF16)

    def tok(d):
        back = lax.rem(j - d + NX * NL, NX * NL)
        return send(tokens.at[back], tokens.at[back], ts.at[d], tr.at[d], at_tp(d))

    def tok_start(d, carry):
        send(tokens.at[j], tokens.at[j], ts.at[d], tr.at[d], at_tp(d)).start()
        return carry

    lax.fori_loop(1, NX * NL, tok_start, 0)

    inner = head_total(gp * agg.astype(F32))
    at = lane(piece)
    stats[z, y, c] = jnp.where(at < 32, top, jnp.where(at < 64, inv, inner))
    g_start(stats, 1)

    def mid(i, carry):
        @pl.when(i < NZ)
        def _():
            g_pass_y(stats, 1, i)

        @pl.when(i >= 1)
        def _():
            g_pass_c(grads, 0, i - 1)
            g_pass_c(stats, 1, i - 1)

        return carry

    def tok_wait(d, carry):
        tok(d).wait_recv()
        return carry

    lax.fori_loop(1, NX * NL, tok_wait, 0)

    tf = tokens[...].reshape(seq, width).astype(F32)
    centred = tf - jnp.mean(tf, axis=1, keepdims=True)
    spread_sq = jnp.mean(centred * centred, axis=1, keepdims=True)
    normed = (centred * lax.rsqrt(spread_sq + 1e-05) * norm_gain[...]).astype(BF16)
    projected = dot(normed, qkv_weight[...]).astype(BF16)
    kv[z, y, c] = projected[:, cols:]
    g_start(kv, 2)
    q = projected[:, 0:cols].astype(F32) * (head_dim ** (-0.5))
    left = iota((seq, cols), 1) < head_dim
    queries[0:seq] = jnp.where(left, q, 0.0).astype(BF16)
    queries[seq:] = jnp.where(left, 0.0, q).astype(BF16)
    run_top[...] = jnp.full_like(run_top, NEG)
    run_sum[...] = jnp.zeros_like(run_sum)
    run_acc[...] = jnp.zeros_like(run_acc)

    lax.fori_loop(0, NZ + 1, mid, 0)

    def mid_take(k, carry):
        g_take(grads, 0, k)
        g_take(stats, 1, k)
        return carry

    lax.fori_loop(0, NZ, mid_take, 0)

    st = stats[...].reshape(rows, LANES)
    at = lane(rows)

    def group(lo):
        kept = jnp.where((at >= lo) & (at < lo + 32), st, 0.0)
        kept = kept + pltpu.roll(kept, 64, 1)
        return kept + pltpu.roll(kept, 32, 1)

    tops[...] = group(0)
    invs[...] = group(32)
    inners[...] = group(64)

    def attend(k):
        zk = lax.rem(z - near(k) + NZ, NZ)
        block = kv[zk].reshape(NY * NC * seq, 2 * cols)
        logits = dot_nt(queries[...], block[:, 0:cols])
        top = jnp.maximum(run_top[...], jnp.max(logits, axis=1, keepdims=True))
        scale = jnp.exp(run_top[...] - top)
        weights = jnp.exp(logits - top[:, 0:1])
        run_sum[...] = run_sum[...] * scale + jnp.sum(weights, axis=1, keepdims=True)
        run_acc[...] = run_acc[...] * scale + dot(weights.astype(BF16), block[:, cols:])
        run_top[...] = top

    def x_send(s, d):
        return send(gterm.at[s, lax.rem(x + d, NX)], x_in.at[s, d], rs.at[s, d], rr.at[s, d], at_x(d))

    def backward(s):
        half = rows // 2

        def part_of(i, carry):
            r0 = pl.multiple_of(i * half, half)
            at = pl.ds(r0, half)
            ge = grads[pl.ds(i * (NZ // 2), NZ // 2)].reshape(half, width).astype(F32)
            probs = jnp.exp(scores[s, at, :] - tops[at, :]) * invs[at, :]
            slot_inner = head_total(values[s, at, :] * ge)
            ds = probs * (slot_inner - inners[at, :])
            ds = jnp.where(lane(half) < heads, ds, 0.0).astype(BF16)
            dvalue[...] = (wide(probs, width) * ge).astype(BF16)
            dembed[at, :] = (dot_nt(dvalue[...], wvp[...]) + dot_nt(ds, kq_rep[...])).astype(BF16)
            return carry

        lax.fori_loop(0, 2, part_of, 0)
        wx = width // NX
        for i in range(NX):
            gterm[s, i] = dot(patches[s], dembed[:, i * wx : (i + 1) * wx])
        for d in range(1, NX):
            x_send(s, d).start()

    def tail(i, carry):
        @pl.when(i < slots)
        def _():
            backward(i)

        @pl.when(i < NZ // 2)
        def _():
            g_pass_y(kv, 2, 2 * i)
            g_pass_y(kv, 2, 2 * i + 1)

        @pl.when((i >= 1) & (i < NZ // 2 + 1))
        def _():
            g_pass_c(kv, 2, 2 * i - 2)
            g_pass_c(kv, 2, 2 * i - 1)

        @pl.when(i >= 2)
        def _():
            for e in (4, 3):
                g_take(kv, 2, 2 * i - e)
                attend(2 * i - e)

        return carry

    lax.fori_loop(0, NZ // 2 + 2, tail, 0)

    def l_send(s):
        return send(l_out.at[s], l_in.at[s], rs.at[s, 0], rr.at[s, 0], l_mate)

    mine = pl.multiple_of(w * cols, cols)
    other = pl.multiple_of((1 - w) * cols, cols)

    def x_sum(s, carry):
        for d in range(1, NX):
            x_send(s, d).wait_recv()
        l_out[s] = gterm[s, x, :, pl.ds(other, cols)] + (
            x_in[s, 1, :, pl.ds(other, cols)] + x_in[s, 2, :, pl.ds(other, cols)] + x_in[s, 3, :, pl.ds(other, cols)]
        )
        embed_grad[s] = gterm[s, x, :, pl.ds(mine, cols)] + (
            x_in[s, 1, :, pl.ds(mine, cols)] + x_in[s, 2, :, pl.ds(mine, cols)] + x_in[s, 3, :, pl.ds(mine, cols)]
        )
        l_send(s).start()
        return carry

    lax.fori_loop(0, slots, x_sum, 0)

    mixed = run_acc[...] / run_sum[...]
    mixed = jnp.where(left, mixed[0:seq], mixed[seq:])
    own = tokens[:, :, pl.ds(pl.multiple_of(j * cols, cols), cols)].reshape(seq, cols)
    layer_out[...] = own.astype(F32) + mixed

    def l_sum(s, carry):
        l_send(s).wait_recv()
        embed_grad[s] = embed_grad[s] + l_in[s]
        return carry

    lax.fori_loop(0, slots, l_sum, 0)

    def b_drain(k, carry):
        b_c(k).wait_send()
        b_y(k).wait_send()

        @pl.when(k < NZ - 1)
        def _():
            b_z(k).wait_send()

        return carry

    lax.fori_loop(0, NZ, b_drain, 0)
    g_drain(grads, 0)
    g_drain(stats, 1)
    g_drain(kv, 2)

    def tok_drain(d, carry):
        tok(d).wait_send()
        return carry

    lax.fori_loop(1, NX * NL, tok_drain, 0)

    def r_drain(s, carry):
        for d in range(1, NX):
            x_send(s, d).wait_send()
        l_send(s).wait_send()
        return carry

    lax.fori_loop(0, slots, r_drain, 0)


def per_device(
    patches,
    slot_weight,
    slot_bias,
    var_embed,
    owner_count,
    slot_variable,
    key_query,
    value_weight,
    norm_gain,
    qkv_weight,
    token_grad,
):
    slots, pixels, rows = patches.shape
    width = value_weight.shape[0]
    piece = token_grad.shape[0]
    cols = qkv_weight.shape[2]
    seq = NX * NL * piece
    zy = (NZ, NY, NC)
    mw = width + LANES
    dma = pltpu.SemaphoreType.DMA
    vm = pltpu.VMEM
    scratch = [
        vm((width, width), BF16),
        vm((width, width), BF16),
        vm((width, LANES), BF16),
        vm((slots, rows, width), BF16),
        vm((slots, rows, width), F32),
        vm((slots, rows, LANES), F32),
        vm((slots, rows, LANES), F32),
        vm((NZ, NY, NC, piece, mw), F32),
        vm((NZ, NY, piece, mw), F32),
        vm((NZ, piece, mw), F32),
        vm((NZ, piece, mw), F32),
        vm((NZ, piece, mw), F32),
        vm((NZ, piece, mw), F32),
        vm(zy + (piece, width), GRAD_T),
        vm(zy + (piece, LANES), F32),
        vm((rows, LANES), F32),
        vm((rows, LANES), F32),
        vm((rows, LANES), F32),
        vm((NX * NL, piece, width), BF16),
        vm((2 * seq, cols), BF16),
        vm(zy + (seq, 2 * cols), BF16),
        vm((2 * seq, LANES), F32),
        vm((2 * seq, LANES), F32),
        vm((2 * seq, cols), F32),
        vm((rows // 2, width), BF16),
        vm((rows, width), BF16),
        vm((slots, NX, pixels, width // NX), F32),
        vm((slots, NX, pixels, width // NX), F32),
        vm((slots, pixels, cols), F32),
        vm((slots, pixels, cols), F32),
        dma((3, NZ)),
        dma((3, NZ)),
        dma((3, 3 * NZ)),
        dma((3, 3 * NZ)),
        dma((NX * NL,)),
        dma((NX * NL,)),
        dma((slots, NX)),
        dma((slots, NX)),
    ]
    in_vm = pl.BlockSpec(memory_space=pltpu.VMEM)
    in_sm = pl.BlockSpec(memory_space=pltpu.SMEM)
    return pl.pallas_call(
        kernel,
        out_shape=(
            jax.ShapeDtypeStruct((seq, cols), F32),
            jax.ShapeDtypeStruct((slots, pixels, cols), F32),
        ),
        in_specs=[in_vm] * 4 + [in_sm] * 2 + [in_vm] * 5,
        out_specs=(in_vm, in_vm),
        scratch_shapes=scratch,
        compiler_params=pltpu.CompilerParams(
            collective_id=0, has_side_effects=True, vmem_limit_bytes=60 * 2**20
        ),
        name="sublayer",
    )(
        patches,
        slot_weight,
        slot_bias,
        var_embed,
        owner_count,
        slot_variable,
        key_query,
        value_weight,
        norm_gain.reshape(1, width),
        qkv_weight.reshape(width, 3 * cols),
        token_grad,
    )


def solution(mesh):
    in_specs = (
        P("var", None, "tp"),
        P("var", None, None),
        P("var", None),
        P(),
        P("var"),
        P("var"),
        P(),
        P(),
        P(),
        P(None, None, "tp"),
        P(("var", "tp"), None),
    )
    out_specs = (P("var", "tp"), P("var", None, "tp"))
    return jax.shard_map(
        per_device, mesh=mesh, in_specs=in_specs, out_specs=out_specs, check_vma=False
    )
```

```python
import functools

import jax
import jax.numpy as jnp
from jax import lax
from jax.experimental import pallas as pl
from jax.experimental.pallas import tpu as pltpu
from jax.sharding import PartitionSpec as P

F32 = jnp.float32
BF16 = jnp.bfloat16
MESH = pl.DeviceIdType.MESH
LANES = 128
NEG = float("-inf")
NZ, NY, NC = 8, 2, 2
NX, NL = 4, 2
HOPS = (2, 5, 8, 11)


def iota(shape, axis):
    return lax.broadcasted_iota(jnp.int32, shape, axis)


def near(k):
    return jnp.where(lax.rem(k, 2) == 1, (k + 1) // 2, lax.rem(NZ - k // 2, NZ))


def far(k):
    return jnp.where(lax.rem(k, 2) == 0, NZ // 2 + k // 2, NZ // 2 - 1 - k // 2)


def dot(a, b):
    return jnp.dot(a, b, preferred_element_type=F32)


def dot_nt(a, b):
    return lax.dot_general(a, b, (((1,), (1,)), ((), ())), preferred_element_type=F32)


def dot_tn(a, b):
    return lax.dot_general(a, b, (((0,), (0,)), ((), ())), preferred_element_type=F32)


def lane(rows):
    return iota((rows, LANES), 1)


def unpack_two(x):
    left = lane(x.shape[0]) < 64
    turned = pltpu.roll(x, 64, 1)
    return jnp.where(left, x, turned), jnp.where(left, turned, x)


def head_total(x):
    total = x[:, 0:LANES]
    for i in range(1, x.shape[1] // LANES):
        total = total + x[:, i * LANES : (i + 1) * LANES]
    for shift in (64, 32, 16):
        total = total + pltpu.roll(total, shift, 1)
    return total


def wide(x, width):
    return jnp.concatenate([x] * (width // LANES), axis=1)


def packed_two(top, total):
    return jnp.where(lane(top.shape[0]) < 64, top, total)


def thirds(x):
    a = x.astype(BF16).astype(F32)
    b = (x - a).astype(BF16).astype(F32)
    return a, b, x - a - b


def packed_six(top, total):
    at = lane(top.shape[0]) // 16
    t1, t2, t3 = thirds(top)
    l1, l2, l3 = thirds(total)
    out = jnp.where(at == 0, t2, jnp.where(at == 1, t1, jnp.where(at == 2, t3, 0.0)))
    return jnp.where(at == 4, l2, jnp.where(at == 5, l1, jnp.where(at == 6, l3, out))).astype(BF16)


def unpack_six(x):
    x = x.astype(F32)
    left = lane(x.shape[0]) < 64

    def whole(kept):
        for shift in (64, 32, 16):
            kept = kept + pltpu.roll(kept, shift, 1)
        return kept

    return whole(jnp.where(left, x, 0.0)), whole(jnp.where(left, 0.0, x))


def merged(first, second):
    s1, m1, l1 = first
    s2, m2, l2 = second
    width = s1.shape[1]
    top = jnp.maximum(m1, m2)
    e1, e2 = jnp.exp(m1 - top), jnp.exp(m2 - top)
    return s1 * wide(e1, width) + s2 * wide(e2, width), top, l1 * e1 + l2 * e2


def kernel(
    patches_hbm,
    slot_weight_hbm,
    slot_bias,
    var_embed_hbm,
    owner_count,
    slot_variable,
    key_query,
    value_weight_hbm,
    norm_gain,
    qkv_weight_hbm,
    token_grad,
    layer_out,
    embed_grad,
    patches,
    slot_weight,
    var_embed,
    value_weight,
    qkv_weight,
    perm,
    wvp,
    kq_rep,
    emb,
    values,
    scores,
    raw,
    part,
    sib_in,
    own,
    y_out,
    y_in,
    z_out,
    z_in,
    grads,
    slot_inner,
    stats,
    tops,
    invs,
    inners,
    tokens,
    queries,
    q_pair,
    kv,
    acc_out,
    acc_in,
    ml_out,
    ml_in,
    run_top,
    run_sum,
    run_acc,
    dvalue,
    dembed,
    gterm,
    x_in,
    l_out,
    l_in,
    bs,
    br,
    gs,
    gr,
    er,
    ts,
    tr,
    rs,
    rr,
    ls,
    ps,
    pr,
):
    slots, pixels, rows = patches.shape
    width = value_weight.shape[0]
    heads = key_query.shape[0]
    piece = token_grad.shape[0]
    head_dim = width // heads
    seq = tokens.shape[0] * piece
    cols = layer_out.shape[1]
    zrows = rows // NZ

    v, j = lax.axis_index("var"), lax.axis_index("tp")
    z, y, c = v // 4, lax.rem(v // 2, 2), lax.rem(v, 2)
    x, w = j // 2, lax.rem(j, 2)

    def at_z(dz):
        return {"var": lax.rem(z + dz, NZ) * 4 + y * 2 + c, "tp": j}

    y_mate = {"var": z * 4 + (1 - y) * 2 + c, "tp": j}
    c_mate = {"var": z * 4 + y * 2 + (1 - c), "tp": j}
    l_mate = {"var": v, "tp": x * 2 + (1 - w)}

    def at_tp(d):
        return {"var": v, "tp": lax.rem(j + d, NX * NL)}

    def at_x(d):
        return {"var": v, "tp": lax.rem(x + d, NX) * 2 + w}

    def send(src, dst, ssem, rsem, device):
        return pltpu.make_async_remote_copy(
            src_ref=src, dst_ref=dst, send_sem=ssem, recv_sem=rsem, device_id=device, device_id_type=MESH
        )

    barrier = pltpu.get_barrier_semaphore()

    def greet_z(d, carry):
        pl.semaphore_signal(barrier, inc=1, device_id=at_z(d), device_id_type=MESH)
        return carry

    def greet_tp(d, carry):
        pl.semaphore_signal(barrier, inc=1, device_id=at_tp(d), device_id_type=MESH)
        return carry

    lax.fori_loop(1, NZ, greet_z, 0)
    lax.fori_loop(1, NX * NL, greet_tp, 0)
    pl.semaphore_signal(barrier, inc=1, device_id=y_mate, device_id_type=MESH)
    pl.semaphore_signal(barrier, inc=1, device_id=c_mate, device_id_type=MESH)

    pairs = (
        (value_weight_hbm, value_weight),
        (patches_hbm, patches),
        (slot_weight_hbm, slot_weight),
        (var_embed_hbm, var_embed),
        (qkv_weight_hbm, qkv_weight),
    )
    loads = [pltpu.make_async_copy(src, dst, ls.at[i]) for i, (src, dst) in enumerate(pairs)]
    for load in loads:
        load.start()

    def g_start(buf, n, rsem):
        mine = buf.at[z, y, c]

        def one(k, carry):
            send(mine, mine, gs.at[n, 0], rsem(k), at_z(near(k))).start()
            return carry

        lax.fori_loop(1, NZ, one, 0)

    def all_z(buf, n, rsem):
        here = buf.at[pl.ds(0, NZ - 1), y, c]
        return send(here, here, gs.at[n, 0], rsem, at_z(1))

    def all_y(buf, n):
        here = buf.at[pl.ds(0, NZ), y, c]
        return send(here, here, gs.at[n, 1], gr.at[n, 1], y_mate)

    def all_c(buf, n):
        here = buf.at[pl.ds(0, NZ), pl.ds(0, NY), c]
        return send(here, here, gs.at[n, 2], gr.at[n, 2], c_mate)

    def z_of(k):
        return lax.rem(z - near(k) + NZ, NZ)

    def kv_z(k):
        here = kv.at[z_of(k), c]
        return send(here, here, gs.at[2, 0], er.at[0, k], at_z(near(k)))

    def kv_c(k):
        here = kv.at[z_of(k), c]
        return send(here, here, gs.at[2, 1], er.at[1, k], c_mate)

    def kv_pass(k):
        kv_z(k).wait_recv()
        kv_c(k).start()

    def q_send():
        return send(q_pair.at[y], q_pair.at[y], ps.at[0], pr.at[0], y_mate)

    def back_send(src, dst, n):
        return send(src, dst, ps.at[n], pr.at[n], y_mate)

    def grad_y():
        here = grads.at[z, y, c]
        return send(here, here, gs.at[0, 1], gr.at[0, 1], y_mate)

    def grad_z(k, to, dz):
        here = grads.at[z_of(k), pl.ds(0, NY), c]
        return send(here, here, gs.at[0, 0], er.at[2, to], at_z(dz))

    def grad_c(k):
        here = grads.at[z_of(k), pl.ds(0, NY), c]
        return send(here, here, gs.at[0, 2], gr.at[0, 2], c_mate)

    def grad_pass(k):
        grad_z(k, k, 1).wait_recv()
        if k <= NZ - 3:
            grad_z(k, k + 2, 1 if k % 2 else NZ - 1).start()
        grad_c(k).start()

    def grad_first():
        grad_y().wait_recv()
        grad_z(0, 1, 1).start()
        grad_z(0, 2, NZ - 1).start()
        grad_c(0).start()

    def all_grad_c():
        here = grads.at[pl.ds(0, NZ), pl.ds(0, NY), c]
        return send(here, here, gs.at[0, 2], gr.at[0, 2], c_mate)

    def grad_hop(n):
        for k in (2 * n + 1, 2 * n + 2):
            if k < NZ:
                grad_pass(k)

    loads[0].wait()

    def make_perm(i, carry):
        cb = pl.multiple_of(i * 256, 256)
        row, col = iota((width, 256), 0), iota((width, 256), 1) + cb
        hit = lax.rem(row, head_dim) * heads + row // head_dim == col
        block = jnp.where(hit, 1.0, 0.0).astype(BF16)
        perm[:, pl.ds(cb, 256)] = block
        wvp[:, pl.ds(cb, 256)] = dot(value_weight[...], block).astype(BF16)
        return carry

    lax.fori_loop(0, width // 256, make_perm, 0)

    g1, g2, g3 = thirds(token_grad[...])
    gp = dot(jnp.concatenate([g1, g2, g3], axis=0).astype(BF16), perm[...])
    gp = gp[0:piece] + (gp[piece : 2 * piece] + gp[2 * piece :])
    grads[z, y, c] = gp

    pl.semaphore_wait(barrier, NZ - 1 + NX * NL - 1 + 2)
    grad_y().start()

    spread = jnp.where(lax.rem(iota((heads, LANES), 1), heads) == iota((heads, LANES), 0), 1.0, 0.0).astype(BF16)
    kq_rep[...] = dot_tn(key_query[...], spread).astype(BF16)

    for load in loads[1:4]:
        load.wait()
    for s in range(slots):
        offset = slot_bias[s : s + 1, :] + var_embed[pl.ds(slot_variable[s], 1), :]
        emb[s] = (dot_tn(patches[s], slot_weight[s]) + offset).astype(BF16)
        bias = jnp.where(s < owner_count[0], 0.0, NEG)
        scores[s] = dot(emb[s], kq_rep[...]) + bias
    top = scores[0]
    for s in range(1, slots):
        top = jnp.maximum(top, scores[s])
    total = jnp.zeros_like(top)
    for s in range(slots):
        e = jnp.exp(scores[s] - top)
        raw[s] = e
        total = total + e
    tops[...] = top
    invs[...] = total
    grad_first()

    def b_c(k):
        return send(part.at[k, pl.ds(0, NY), 1 - c], sib_in.at[k], bs.at[0], br.at[0, k], c_mate)

    def b_y(k):
        return send(y_out.at[k], y_in.at[k], bs.at[1], br.at[1, k], y_mate)

    def b_z(k):
        return send(z_out.at[k], z_in.at[k], bs.at[2], br.at[2, 0], at_z(far(k)))

    def all_b_z():
        return send(z_out.at[pl.ds(0, NZ - 1)], z_in.at[pl.ds(0, NZ - 1)], bs.at[2], br.at[2, 0], at_z(1))

    def first_stage(k):
        start = pl.multiple_of(lax.rem(z + far(k), NZ) * zrows, zrows)
        e = emb[:, pl.ds(start, zrows), :].reshape(slots * zrows, width)
        val = dot(e, wvp[...]).reshape(slots, zrows, width)
        values[:, pl.ds(start, zrows), :] = val
        for i in range(width // LANES):
            at = slice(i * LANES, (i + 1) * LANES)
            acc = raw[0, pl.ds(start, zrows), :] * val[0, :, at]
            for s in range(1, slots):
                acc = acc + raw[s, pl.ds(start, zrows), :] * val[s, :, at]
            part[k, :, :, :, at] = acc.reshape(NY, NC, piece, LANES)
        both = packed_two(tops[pl.ds(start, zrows), :], invs[pl.ds(start, zrows), :])
        part[k, :, :, :, width:] = both.reshape(NY, NC, piece, LANES)
        b_c(k).start()

    def both_of(ref):
        return (ref[:, 0:width], *unpack_two(ref[:, width:]))

    def six_of(ref):
        return (ref[:, 0:width].astype(F32), *unpack_six(ref[:, width:]))

    def second_stage(k):
        b_c(k).wait_recv()
        sums, m, l = merged(both_of(part.at[k, 1 - y, c]), both_of(sib_in.at[k, 1 - y]))
        y_out[k, :, 0:width] = sums
        y_out[k, :, width:] = packed_two(m, l)
        b_y(k).start()
        sums, m, l = merged(both_of(part.at[k, y, c]), both_of(sib_in.at[k, y]))
        own[k, :, 0:width] = sums
        own[k, :, width:] = packed_two(m, l)

    def third_stage(k):
        b_y(k).wait_recv()
        sums, m, l = merged(both_of(own.at[k]), both_of(y_in.at[k]))

        @pl.when(k < NZ - 1)
        def _():
            z_out[k, :, 0:width] = sums.astype(BF16)
            z_out[k, :, width:] = packed_six(m, l)
            b_z(k).start()

        @pl.when(k == NZ - 1)
        def _():
            own[k, :, 0:width] = sums
            own[k, :, width:] = packed_two(m, l)

    def step(i, carry):
        @pl.when(i < NZ)
        def _():
            first_stage(i)

        @pl.when((i >= 2) & (i < NZ + 2))
        def _():
            second_stage(i - 2)

        @pl.when(i >= 4)
        def _():
            third_stage(i - 4)

        for n in range(NZ // 2):
            pl.when(i == HOPS[n])(functools.partial(grad_hop, n))
        return carry

    lax.fori_loop(0, NZ + 4, step, 0)

    all_b_z().wait_recv()
    terms = [both_of(own.at[NZ - 1])] + [six_of(z_in.at[k]) for k in range(NZ - 1)]
    top = functools.reduce(jnp.maximum, [m for _, m, _ in terms])
    es = [jnp.exp(m - top) for _, m, _ in terms]
    total = functools.reduce(jnp.add, [l * e for (_, _, l), e in zip(terms, es)])
    sums = functools.reduce(jnp.add, [t * wide(e, width) for (t, _, _), e in zip(terms, es)])
    agg = (sums / wide(total, width)).astype(BF16)
    tokens[j] = dot_nt(agg, perm[...]).astype(BF16)

    def tok(d):
        return send(tokens.at[j], tokens.at[j], ts.at[0], tr.at[0], at_tp(d))

    def all_tok():
        here = tokens.at[pl.ds(0, NX * NL - 1)]
        return send(here, here, ts.at[0], tr.at[0], at_tp(1))

    def tok_start(d, carry):
        tok(d).start()
        return carry

    lax.fori_loop(1, NX * NL, tok_start, 0)

    inner = head_total(gp * agg.astype(F32))
    at = lane(piece)
    stats[z, y, c] = jnp.where(at < 32, top, jnp.where(at < 64, total, inner))
    g_start(stats, 1, lambda k: gr.at[1, 0])

    half = rows // 2

    def inner_of(h):
        at = slice(h * half, (h + 1) * half)

        def one(s, carry):
            ge = grads[h * (NZ // 2) : (h + 1) * (NZ // 2)].reshape(half, width)
            slot_inner[s, at, :] = head_total(values[s, at, :] * ge)
            return carry

        lax.fori_loop(0, slots, one, 0)

    all_grad_c().wait_recv()
    inner_of(0)
    inner_of(1)
    all_tok().wait_recv()
    loads[4].wait()

    tf = tokens[...].reshape(seq, width).astype(F32)
    centred = tf - jnp.mean(tf, axis=1, keepdims=True)
    spread_sq = jnp.mean(centred * centred, axis=1, keepdims=True)
    normed = (centred * lax.rsqrt(spread_sq + 1e-05) * norm_gain[...]).astype(BF16)
    all_qkv = jnp.concatenate([qkv_weight[i] for i in range(3)], axis=1)
    projected = dot(normed, all_qkv).astype(BF16)
    mine = kv.at[z, c]
    mine[...] = projected[:, cols:]

    def kv_start(k, carry):
        send(mine, mine, gs.at[2, 0], er.at[0, k], at_z(near(k))).start()
        return carry

    lax.fori_loop(1, NZ, kv_start, 0)
    q_pair[y] = projected[:, 0:cols]
    q_send().start()
    kv_c(0).start()
    left = iota((seq, cols), 1) < head_dim

    def both_heads(q):
        q = q.astype(F32) * (head_dim ** (-0.5))
        return jnp.where(left, q, 0.0).astype(BF16), jnp.where(left, 0.0, q).astype(BF16)

    queries[0:seq], queries[seq : 2 * seq] = both_heads(projected[:, 0:cols])
    run_top[...] = jnp.full_like(run_top, NEG)
    run_sum[...] = jnp.zeros_like(run_sum)
    run_acc[...] = jnp.zeros_like(run_acc)
    def attend(k):
        block = kv[z_of(k)].reshape(NC * seq, 2 * cols)
        logits = dot_nt(queries[...], block[:, 0:cols])
        top = jnp.maximum(run_top[...], jnp.max(logits, axis=1, keepdims=True))
        scale = jnp.exp(run_top[...] - top)
        weights = jnp.exp(logits - top[:, 0:1])
        run_sum[...] = run_sum[...] * scale + jnp.sum(weights, axis=1, keepdims=True)
        run_acc[...] = run_acc[...] * scale + dot(weights.astype(BF16), block[:, cols:])
        run_top[...] = top

    all_z(stats, 1, gr.at[1, 0]).wait_recv()
    all_y(stats, 1).start()
    q_send().wait_recv()
    queries[2 * seq : 3 * seq], queries[3 * seq :] = both_heads(q_pair[1 - y])
    kv_c(0).wait_recv()
    attend(0)
    all_y(stats, 1).wait_recv()
    all_c(stats, 1).start()
    all_c(stats, 1).wait_recv()

    st = stats[...].reshape(rows, LANES)
    at = lane(rows)

    def group(lo):
        kept = jnp.where((at >= lo) & (at < lo + 32), st, 0.0)
        kept = kept + pltpu.roll(kept, 64, 1)
        return kept + pltpu.roll(kept, 32, 1)

    tops[...] = group(0)
    invs[...] = 1.0 / group(32)
    inners[...] = group(64)

    def x_send(s, d):
        return send(gterm.at[s, lax.rem(x + d, NX)], x_in.at[s, d], rs.at[0], rr.at[0, s], at_x(d))

    def all_x(s):
        return send(gterm.at[s, pl.ds(0, NX - 1)], x_in.at[s, pl.ds(1, NX - 1)], rs.at[0], rr.at[0, s], at_x(1))

    def backward(s):
        def part_of(i, carry):
            at = pl.ds(pl.multiple_of(i * half, half), half)
            ge = grads[pl.ds(i * (NZ // 2), NZ // 2)].reshape(half, width)
            probs = jnp.exp(scores[s, at, :] - tops[at, :]) * invs[at, :]
            ds = probs * (slot_inner[s, at, :] - inners[at, :])
            ds = jnp.where(lane(half) < heads, ds, 0.0).astype(BF16)
            dvalue[...] = (wide(probs, width) * ge).astype(BF16)
            dembed[at, :] = (dot_nt(dvalue[...], wvp[...]) + dot_nt(ds, kq_rep[...])).astype(BF16)
            return carry

        lax.fori_loop(0, 2, part_of, 0)
        wx = width // NX
        for i in range(NX):
            term = dot(patches[s], dembed[:, i * wx : (i + 1) * wx])
            gterm[s, i] = term
        for d in range(1, NX):
            x_send(s, d).start()

    def slot_step(s, carry):
        backward(s)
        kv_pass(2 * s + 1)

        @pl.when(s < slots - 1)
        def _():
            kv_pass(2 * s + 2)

        return carry

    lax.fori_loop(0, slots, slot_step, 0)

    def key_step(k, carry):
        kv_c(k).wait_recv()
        attend(k)
        return carry

    lax.fori_loop(1, NZ, key_step, 0)

    acc_out[...] = jnp.where(left, run_acc[2 * seq : 3 * seq], run_acc[3 * seq :])
    at = lane(seq)
    table = jnp.where(at == 0, run_top[2 * seq : 3 * seq], run_top[3 * seq :])
    table = jnp.where(at == 2, run_sum[2 * seq : 3 * seq], jnp.where(at == 3, run_sum[3 * seq :], table))
    ml_out[...] = table.T[0:8]
    back_send(acc_out, acc_in, 1).start()
    back_send(ml_out, ml_in, 2).start()

    def l_send(s):
        return send(l_out.at[s], l_in.at[s], rs.at[1], rr.at[1, s], l_mate)

    near_col = pl.multiple_of(w * cols, cols)
    other = pl.multiple_of((1 - w) * cols, cols)

    def x_sum(s, carry):
        all_x(s).wait_recv()

        def summed(at):
            terms = [x_in[s, d, :, pl.ds(at, cols)] for d in range(1, NX)]
            return gterm[s, x, :, pl.ds(at, cols)] + (terms[0] + terms[1] + terms[2])

        l_out[s] = summed(other)
        l_send(s).start()
        embed_grad[s] = summed(near_col)
        return carry

    lax.fori_loop(0, slots, x_sum, 0)

    back_send(acc_out, acc_in, 1).wait_recv()
    back_send(ml_out, ml_in, 2).wait_recv()
    table = jnp.concatenate([ml_in[...], jnp.zeros((seq - 8, seq), F32)], axis=0).T
    m1 = jnp.where(left, run_top[0:seq], run_top[seq : 2 * seq])
    l1 = jnp.where(left, run_sum[0:seq], run_sum[seq : 2 * seq])
    a1 = jnp.where(left, run_acc[0:seq], run_acc[seq : 2 * seq])
    m2 = jnp.where(left, table[:, 0:1], table[:, 1:2])
    l2 = jnp.where(left, table[:, 2:3], table[:, 3:4])
    top = jnp.maximum(m1, m2)
    e1, e2 = jnp.exp(m1 - top), jnp.exp(m2 - top)
    mixed = (a1 * e1 + acc_in[...] * e2) / (l1 * e1 + l2 * e2)
    kept = tokens[:, :, pl.ds(pl.multiple_of(j * cols, cols), cols)].reshape(seq, cols)
    layer_out[...] = kept.astype(F32) + mixed

    def l_sum(s, carry):
        l_send(s).wait_recv()
        embed_grad[s] = embed_grad[s] + l_in[s]
        return carry

    lax.fori_loop(0, slots, l_sum, 0)

    send(part.at[pl.ds(0, NZ), pl.ds(0, NY), 1 - c], sib_in, bs.at[0], br.at[0, 0], c_mate).wait_send()
    send(y_out, y_in, bs.at[1], br.at[1, 0], y_mate).wait_send()
    all_b_z().wait_send()
    all_z(stats, 1, gr.at[1, 0]).wait_send()
    all_y(stats, 1).wait_send()
    all_c(stats, 1).wait_send()
    grad_y().wait_send()
    grads_left = grads.at[pl.ds(0, NZ - 1), pl.ds(0, NY), c]
    send(grads_left, grads_left, gs.at[0, 0], er.at[2, 0], at_z(1)).wait_send()
    all_grad_c().wait_send()
    kv_left = kv.at[pl.ds(0, NZ - 1), c]
    send(kv_left, kv_left, gs.at[2, 0], er.at[0, 0], at_z(1)).wait_send()
    kv_left = kv.at[pl.ds(0, NZ), c]
    send(kv_left, kv_left, gs.at[2, 1], er.at[1, 0], c_mate).wait_send()
    q_send().wait_send()
    back_send(acc_out, acc_in, 1).wait_send()
    back_send(ml_out, ml_in, 2).wait_send()
    all_tok().wait_send()
    x_left = gterm.at[pl.ds(0, slots), pl.ds(0, NX - 1)]
    send(x_left, x_left, rs.at[0], rr.at[0, 0], at_x(1)).wait_send()
    send(l_out, l_in, rs.at[1], rr.at[1, 0], l_mate).wait_send()


def per_device(
    patches,
    slot_weight,
    slot_bias,
    var_embed,
    owner_count,
    slot_variable,
    key_query,
    value_weight,
    norm_gain,
    qkv_weight,
    token_grad,
):
    slots, pixels, rows = patches.shape
    width = value_weight.shape[0]
    piece = token_grad.shape[0]
    cols = qkv_weight.shape[2]
    seq = NX * NL * piece
    zy = (NZ, NY, NC)
    mw = width + LANES
    dma = pltpu.SemaphoreType.DMA
    vm = pltpu.VMEM
    scratch = [
        vm((slots, pixels, rows), BF16),
        vm((slots, pixels, width), BF16),
        vm(var_embed.shape, F32),
        vm((width, width), BF16),
        vm((3, width, cols), BF16),
        vm((width, width), BF16),
        vm((width, width), BF16),
        vm((width, LANES), BF16),
        vm((slots, rows, width), BF16),
        vm((slots, rows, width), F32),
        vm((slots, rows, LANES), F32),
        vm((slots, rows, LANES), F32),
        vm((NZ, NY, NC, piece, mw), F32),
        vm((NZ, NY, piece, mw), F32),
        vm((NZ, piece, mw), F32),
        vm((NZ, piece, mw), F32),
        vm((NZ, piece, mw), F32),
        vm((NZ, piece, mw), BF16),
        vm((NZ, piece, mw), BF16),
        vm(zy + (piece, width), F32),
        vm((slots, rows, LANES), F32),
        vm(zy + (piece, LANES), F32),
        vm((rows, LANES), F32),
        vm((rows, LANES), F32),
        vm((rows, LANES), F32),
        vm((NX * NL, piece, width), BF16),
        vm((4 * seq, cols), BF16),
        vm((NY, seq, cols), BF16),
        vm((NZ, NC, seq, 2 * cols), BF16),
        vm((seq, cols), F32),
        vm((seq, cols), F32),
        vm((8, seq), F32),
        vm((8, seq), F32),
        vm((4 * seq, LANES), F32),
        vm((4 * seq, LANES), F32),
        vm((4 * seq, cols), F32),
        vm((rows // 2, width), BF16),
        vm((rows, width), BF16),
        vm((slots, NX, pixels, width // NX), F32),
        vm((slots, NX, pixels, width // NX), F32),
        vm((slots, pixels, cols), F32),
        vm((slots, pixels, cols), F32),
        dma((3,)),
        dma((3, NZ)),
        dma((3, 3)),
        dma((2, 5)),
        dma((3, NZ)),
        dma((1,)),
        dma((1,)),
        dma((2,)),
        dma((2, slots)),
        dma((5,)),
        dma((3,)),
        dma((3,)),
    ]
    in_vm = pl.BlockSpec(memory_space=pltpu.VMEM)
    in_hbm = pl.BlockSpec(memory_space=pl.ANY)
    in_sm = pl.BlockSpec(memory_space=pltpu.SMEM)
    return pl.pallas_call(
        kernel,
        out_shape=(
            jax.ShapeDtypeStruct((seq, cols), F32),
            jax.ShapeDtypeStruct((slots, pixels, cols), F32),
        ),
        in_specs=[in_hbm, in_hbm, in_vm, in_hbm, in_sm, in_sm, in_vm, in_hbm, in_vm, in_hbm, in_vm],
        out_specs=(in_vm, in_vm),
        scratch_shapes=scratch,
        compiler_params=pltpu.CompilerParams(
            collective_id=0, has_side_effects=True, vmem_limit_bytes=60 * 2**20
        ),
        name="sublayer",
    )(
        patches,
        slot_weight,
        slot_bias,
        var_embed,
        owner_count,
        slot_variable,
        key_query.T,
        value_weight,
        norm_gain.reshape(1, width),
        qkv_weight.transpose(1, 0, 2),
        token_grad,
    )


def solution(mesh):
    in_specs = (
        P("var", None, "tp"),
        P("var", None, None),
        P("var", None),
        P(),
        P("var"),
        P("var"),
        P(),
        P(),
        P(),
        P(None, None, "tp"),
        P(("var", "tp"), None),
    )
    out_specs = (P("var", "tp"), P("var", None, "tp"))
    return jax.shard_map(
        per_device, mesh=mesh, in_specs=in_specs, out_specs=out_specs, check_vma=False
    )
```

```python
import functools

import jax
import jax.numpy as jnp
from jax import lax
from jax.experimental import pallas as pl
from jax.experimental.pallas import tpu as pltpu
from jax.sharding import PartitionSpec as P

F32 = jnp.float32
BF16 = jnp.bfloat16
MESH = pl.DeviceIdType.MESH
LANES = 128
NEG = float("-inf")
NZ, NY, NC = 8, 2, 2
NX, NL = 4, 2
HOPS = (2, 5, 8, 11)
FAR = 3


def iota(shape, axis):
    return lax.broadcasted_iota(jnp.int32, shape, axis)


def near(k):
    return jnp.where(lax.rem(k, 2) == 1, (k + 1) // 2, lax.rem(NZ - k // 2, NZ))


def far(k):
    return jnp.where(lax.rem(k, 2) == 0, NZ // 2 + k // 2, NZ // 2 - 1 - k // 2)


def dot(a, b):
    return jnp.dot(a, b, preferred_element_type=F32)


def dot_nt(a, b):
    return lax.dot_general(a, b, (((1,), (1,)), ((), ())), preferred_element_type=F32)


def dot_tn(a, b):
    return lax.dot_general(a, b, (((0,), (0,)), ((), ())), preferred_element_type=F32)


def lane(rows):
    return iota((rows, LANES), 1)


def unpack_two(x):
    left = lane(x.shape[0]) < 64
    turned = pltpu.roll(x, 64, 1)
    return jnp.where(left, x, turned), jnp.where(left, turned, x)


def head_total(x):
    total = x[:, 0:LANES]
    for i in range(1, x.shape[1] // LANES):
        total = total + x[:, i * LANES : (i + 1) * LANES]
    for shift in (64, 32, 16):
        total = total + pltpu.roll(total, shift, 1)
    return total


def wide(x, width):
    return jnp.concatenate([x] * (width // LANES), axis=1)


def packed_two(top, total):
    return jnp.where(lane(top.shape[0]) < 64, top, total)


def thirds(x):
    a = x.astype(BF16).astype(F32)
    b = (x - a).astype(BF16).astype(F32)
    return a, b, x - a - b


def packed_six(top, total):
    at = lane(top.shape[0]) // 16
    t1, t2, t3 = thirds(top)
    l1, l2, l3 = thirds(total)
    out = jnp.where(at == 0, t2, jnp.where(at == 1, t1, jnp.where(at == 2, t3, 0.0)))
    return jnp.where(at == 4, l2, jnp.where(at == 5, l1, jnp.where(at == 6, l3, out))).astype(BF16)


def unpack_six(x):
    x = x.astype(F32)
    left = lane(x.shape[0]) < 64

    def whole(kept):
        for shift in (64, 32, 16):
            kept = kept + pltpu.roll(kept, shift, 1)
        return kept

    return whole(jnp.where(left, x, 0.0)), whole(jnp.where(left, 0.0, x))


def merged(first, second):
    s1, m1, l1 = first
    s2, m2, l2 = second
    width = s1.shape[1]
    top = jnp.maximum(m1, m2)
    e1, e2 = jnp.exp(m1 - top), jnp.exp(m2 - top)
    return s1 * wide(e1, width) + s2 * wide(e2, width), top, l1 * e1 + l2 * e2


def kernel(
    patches_hbm,
    slot_weight_hbm,
    slot_bias,
    var_embed_hbm,
    owner_count,
    slot_variable,
    key_query,
    value_weight_hbm,
    norm_gain,
    qkv_weight_hbm,
    token_grad,
    layer_out,
    embed_grad,
    patches,
    slot_weight,
    var_embed,
    value_weight,
    qkv_weight,
    perm,
    wvp,
    kq_rep,
    emb,
    values,
    scores,
    raw,
    part,
    sib_in,
    own,
    y_out,
    y_in,
    z_out,
    z_in,
    far_out,
    far_in,
    grads,
    slot_inner,
    stats,
    tops,
    invs,
    inners,
    tokens,
    queries,
    q_pair,
    kv,
    acc_out,
    acc_in,
    ml_out,
    ml_in,
    run_top,
    run_sum,
    run_acc,
    dvalue,
    dembed,
    gterm,
    x_in,
    l_out,
    l_in,
    bs,
    br,
    gs,
    gr,
    er,
    ts,
    tr,
    rs,
    rr,
    ls,
    ps,
    pr,
):
    slots, pixels, rows = patches.shape
    width = value_weight.shape[0]
    heads = key_query.shape[0]
    piece = token_grad.shape[0]
    head_dim = width // heads
    seq = tokens.shape[0] * piece
    cols = layer_out.shape[1]
    zrows = rows // NZ

    v, j = lax.axis_index("var"), lax.axis_index("tp")
    z, y, c = v // 4, lax.rem(v // 2, 2), lax.rem(v, 2)
    x, w = j // 2, lax.rem(j, 2)

    def at_z(dz):
        return {"var": lax.rem(z + dz, NZ) * 4 + y * 2 + c, "tp": j}

    y_mate = {"var": z * 4 + (1 - y) * 2 + c, "tp": j}
    c_mate = {"var": z * 4 + y * 2 + (1 - c), "tp": j}
    l_mate = {"var": v, "tp": x * 2 + (1 - w)}

    def at_tp(d):
        return {"var": v, "tp": lax.rem(j + d, NX * NL)}

    def at_x(d):
        return {"var": v, "tp": lax.rem(x + d, NX) * 2 + w}

    def send(src, dst, ssem, rsem, device):
        return pltpu.make_async_remote_copy(
            src_ref=src, dst_ref=dst, send_sem=ssem, recv_sem=rsem, device_id=device, device_id_type=MESH
        )

    barrier = pltpu.get_barrier_semaphore()

    def greet_z(d, carry):
        pl.semaphore_signal(barrier, inc=1, device_id=at_z(d), device_id_type=MESH)
        return carry

    def greet_tp(d, carry):
        pl.semaphore_signal(barrier, inc=1, device_id=at_tp(d), device_id_type=MESH)
        return carry

    lax.fori_loop(1, NZ, greet_z, 0)
    lax.fori_loop(1, NX * NL, greet_tp, 0)
    pl.semaphore_signal(barrier, inc=1, device_id=y_mate, device_id_type=MESH)
    pl.semaphore_signal(barrier, inc=1, device_id=c_mate, device_id_type=MESH)

    pairs = (
        (value_weight_hbm, value_weight),
        (patches_hbm, patches),
        (slot_weight_hbm, slot_weight),
        (var_embed_hbm, var_embed),
        (qkv_weight_hbm, qkv_weight),
    )
    loads = [pltpu.make_async_copy(src, dst, ls.at[i]) for i, (src, dst) in enumerate(pairs)]
    for load in loads:
        load.start()

    def g_start(buf, n, rsem):
        mine = buf.at[z, y, c]

        def one(k, carry):
            send(mine, mine, gs.at[n, 0], rsem(k), at_z(near(k))).start()
            return carry

        lax.fori_loop(1, NZ, one, 0)

    def all_z(buf, n, rsem):
        here = buf.at[pl.ds(0, NZ - 1), y, c]
        return send(here, here, gs.at[n, 0], rsem, at_z(1))

    def all_y(buf, n):
        here = buf.at[pl.ds(0, NZ), y, c]
        return send(here, here, gs.at[n, 1], gr.at[n, 1], y_mate)

    def all_c(buf, n):
        here = buf.at[pl.ds(0, NZ), pl.ds(0, NY), c]
        return send(here, here, gs.at[n, 2], gr.at[n, 2], c_mate)

    def z_of(k):
        return lax.rem(z - near(k) + NZ, NZ)

    def kv_z(k):
        here = kv.at[z_of(k), c]
        return send(here, here, gs.at[2, 0], er.at[0, k], at_z(near(k)))

    def kv_c(k):
        here = kv.at[z_of(k), c]
        return send(here, here, gs.at[2, 1], er.at[1, k], c_mate)

    def kv_pass(k):
        kv_z(k).wait_recv()
        kv_c(k).start()

    def q_send():
        return send(q_pair.at[y], q_pair.at[y], ps.at[0], pr.at[0], y_mate)

    def back_send(src, dst, n):
        return send(src, dst, ps.at[n], pr.at[n], y_mate)

    def grad_y():
        here = grads.at[z, y, c]
        return send(here, here, gs.at[0, 1], gr.at[0, 1], y_mate)

    def grad_z(k, to, dz):
        here = grads.at[z_of(k), pl.ds(0, NY), c]
        return send(here, here, gs.at[0, 0], er.at[2, to], at_z(dz))

    def grad_c(k):
        here = grads.at[z_of(k), pl.ds(0, NY), c]
        return send(here, here, gs.at[0, 2], gr.at[0, 2], c_mate)

    def grad_pass(k):
        grad_z(k, k, 1).wait_recv()
        if k <= NZ - 3:
            grad_z(k, k + 2, 1 if k % 2 else NZ - 1).start()
        grad_c(k).start()

    def grad_first():
        grad_y().wait_recv()
        grad_z(0, 1, 1).start()
        grad_z(0, 2, NZ - 1).start()
        grad_c(0).start()

    def all_grad_c():
        here = grads.at[pl.ds(0, NZ), pl.ds(0, NY), c]
        return send(here, here, gs.at[0, 2], gr.at[0, 2], c_mate)

    def grad_hop(n):
        for k in (2 * n + 1, 2 * n + 2):
            if k < NZ:
                grad_pass(k)

    loads[0].wait()

    def make_perm(i, carry):
        cb = pl.multiple_of(i * 256, 256)
        row, col = iota((width, 256), 0), iota((width, 256), 1) + cb
        hit = lax.rem(row, head_dim) * heads + row // head_dim == col
        block = jnp.where(hit, 1.0, 0.0).astype(BF16)
        perm[:, pl.ds(cb, 256)] = block
        wvp[:, pl.ds(cb, 256)] = dot(value_weight[...], block).astype(BF16)
        return carry

    lax.fori_loop(0, width // 256, make_perm, 0)

    g1, g2, g3 = thirds(token_grad[...])
    gp = dot(jnp.concatenate([g1, g2, g3], axis=0).astype(BF16), perm[...])
    gp = gp[0:piece] + (gp[piece : 2 * piece] + gp[2 * piece :])
    grads[z, y, c] = gp

    pl.semaphore_wait(barrier, NZ - 1 + NX * NL - 1 + 2)
    grad_y().start()

    spread = jnp.where(lax.rem(iota((heads, LANES), 1), heads) == iota((heads, LANES), 0), 1.0, 0.0).astype(BF16)
    kq_rep[...] = dot_tn(key_query[...], spread).astype(BF16)

    for load in loads[1:4]:
        load.wait()
    for s in range(slots):
        offset = slot_bias[s : s + 1, :] + var_embed[pl.ds(slot_variable[s], 1), :]
        emb[s] = (dot_tn(patches[s], slot_weight[s]) + offset).astype(BF16)
        bias = jnp.where(s < owner_count[0], 0.0, NEG)
        scores[s] = dot(emb[s], kq_rep[...]) + bias
    top = scores[0]
    for s in range(1, slots):
        top = jnp.maximum(top, scores[s])
    total = jnp.zeros_like(top)
    for s in range(slots):
        e = jnp.exp(scores[s] - top)
        raw[s] = e
        total = total + e
    tops[...] = top
    invs[...] = total
    grad_first()

    def b_c(k):
        return send(part.at[k, pl.ds(0, NY), 1 - c], sib_in.at[k], bs.at[0], br.at[0, k], c_mate)

    def b_y(k):
        return send(y_out.at[k], y_in.at[k], bs.at[1], br.at[1, k], y_mate)

    def b_z(k):
        return send(z_out.at[k], z_in.at[k], bs.at[2], br.at[2, 0], at_z(far(k)))

    def b_far(k):
        return send(far_out.at[k], far_in.at[k], bs.at[3], br.at[2, 1], at_z(far(k)))

    def all_b_z():
        at = pl.ds(FAR, NZ - 1 - FAR)
        return send(z_out.at[at], z_in.at[at], bs.at[2], br.at[2, 0], at_z(1))

    def all_b_far():
        return send(far_out, far_in, bs.at[3], br.at[2, 1], at_z(1))

    def first_stage(k):
        start = pl.multiple_of(lax.rem(z + far(k), NZ) * zrows, zrows)
        e = emb[:, pl.ds(start, zrows), :].reshape(slots * zrows, width)
        val = dot(e, wvp[...]).reshape(slots, zrows, width)
        values[:, pl.ds(start, zrows), :] = val
        for i in range(width // LANES):
            at = slice(i * LANES, (i + 1) * LANES)
            acc = raw[0, pl.ds(start, zrows), :] * val[0, :, at]
            for s in range(1, slots):
                acc = acc + raw[s, pl.ds(start, zrows), :] * val[s, :, at]
            part[k, :, :, :, at] = acc.reshape(NY, NC, piece, LANES)
        both = packed_two(tops[pl.ds(start, zrows), :], invs[pl.ds(start, zrows), :])
        part[k, :, :, :, width:] = both.reshape(NY, NC, piece, LANES)
        b_c(k).start()

    def both_of(ref):
        return (ref[:, 0:width], *unpack_two(ref[:, width:]))

    def six_of(ref):
        return (ref[:, 0:width].astype(F32), *unpack_six(ref[:, width:]))

    def second_stage(k):
        b_c(k).wait_recv()
        sums, m, l = merged(both_of(part.at[k, 1 - y, c]), both_of(sib_in.at[k, 1 - y]))
        y_out[k, :, 0:width] = sums
        y_out[k, :, width:] = packed_two(m, l)
        b_y(k).start()
        sums, m, l = merged(both_of(part.at[k, y, c]), both_of(sib_in.at[k, y]))
        own[k, :, 0:width] = sums
        own[k, :, width:] = packed_two(m, l)

    def third_stage(k):
        b_y(k).wait_recv()
        sums, m, l = merged(both_of(own.at[k]), both_of(y_in.at[k]))

        @pl.when(k < FAR)
        def _():
            far_out[k, :, 0:width] = sums.astype(BF16)
            far_out[k, :, width:] = packed_six(m, l)
            b_far(k).start()

        @pl.when((k >= FAR) & (k < NZ - 1))
        def _():
            z_out[k, :, 0:width] = sums
            z_out[k, :, width:] = packed_two(m, l)
            b_z(k).start()

        @pl.when(k == NZ - 1)
        def _():
            own[k, :, 0:width] = sums
            own[k, :, width:] = packed_two(m, l)

    def step(i, carry):
        @pl.when(i < NZ)
        def _():
            first_stage(i)

        @pl.when((i >= 2) & (i < NZ + 2))
        def _():
            second_stage(i - 2)

        @pl.when(i >= 4)
        def _():
            third_stage(i - 4)

        for n in range(NZ // 2):
            pl.when(i == HOPS[n])(functools.partial(grad_hop, n))
        return carry

    lax.fori_loop(0, NZ + 4, step, 0)

    all_b_far().wait_recv()
    all_b_z().wait_recv()
    terms = [both_of(own.at[NZ - 1])] + [six_of(far_in.at[k]) for k in range(FAR)]
    terms += [both_of(z_in.at[k]) for k in range(FAR, NZ - 1)]
    top = functools.reduce(jnp.maximum, [m for _, m, _ in terms])
    es = [jnp.exp(m - top) for _, m, _ in terms]
    total = functools.reduce(jnp.add, [l * e for (_, _, l), e in zip(terms, es)])
    sums = functools.reduce(jnp.add, [t * wide(e, width) for (t, _, _), e in zip(terms, es)])
    agg = (sums / wide(total, width)).astype(BF16)
    tokens[j] = dot_nt(agg, perm[...]).astype(BF16)

    def tok(d):
        return send(tokens.at[j], tokens.at[j], ts.at[0], tr.at[0], at_tp(d))

    def all_tok():
        here = tokens.at[pl.ds(0, NX * NL - 1)]
        return send(here, here, ts.at[0], tr.at[0], at_tp(1))

    def tok_start(d, carry):
        tok(d).start()
        return carry

    lax.fori_loop(1, NX * NL, tok_start, 0)

    inner = head_total(gp * agg.astype(F32))
    at = lane(piece)
    stats[z, y, c] = jnp.where(at < 32, top, jnp.where(at < 64, total, inner))
    g_start(stats, 1, lambda k: gr.at[1, 0])

    half = rows // 2

    def inner_of(h):
        at = slice(h * half, (h + 1) * half)

        def one(s, carry):
            ge = grads[h * (NZ // 2) : (h + 1) * (NZ // 2)].reshape(half, width)
            slot_inner[s, at, :] = head_total(values[s, at, :] * ge)
            return carry

        lax.fori_loop(0, slots, one, 0)

    all_grad_c().wait_recv()
    inner_of(0)
    inner_of(1)
    all_tok().wait_recv()
    loads[4].wait()

    tf = tokens[...].reshape(seq, width).astype(F32)
    centred = tf - jnp.mean(tf, axis=1, keepdims=True)
    spread_sq = jnp.mean(centred * centred, axis=1, keepdims=True)
    normed = (centred * lax.rsqrt(spread_sq + 1e-05) * norm_gain[...]).astype(BF16)
    all_qkv = jnp.concatenate([qkv_weight[i] for i in range(3)], axis=1)
    projected = dot(normed, all_qkv).astype(BF16)
    mine = kv.at[z, c]
    mine[...] = projected[:, cols:]

    def kv_start(k, carry):
        send(mine, mine, gs.at[2, 0], er.at[0, k], at_z(near(k))).start()
        return carry

    lax.fori_loop(1, NZ, kv_start, 0)
    q_pair[y] = projected[:, 0:cols]
    q_send().start()
    kv_c(0).start()
    left = iota((seq, cols), 1) < head_dim

    def both_heads(q):
        q = q.astype(F32) * (head_dim ** (-0.5))
        return jnp.where(left, q, 0.0).astype(BF16), jnp.where(left, 0.0, q).astype(BF16)

    queries[0:seq], queries[seq : 2 * seq] = both_heads(projected[:, 0:cols])
    run_top[...] = jnp.full_like(run_top, NEG)
    run_sum[...] = jnp.zeros_like(run_sum)
    run_acc[...] = jnp.zeros_like(run_acc)
    def attend(k):
        block = kv[z_of(k)].reshape(NC * seq, 2 * cols)
        logits = dot_nt(queries[...], block[:, 0:cols])
        top = jnp.maximum(run_top[...], jnp.max(logits, axis=1, keepdims=True))
        scale = jnp.exp(run_top[...] - top)
        weights = jnp.exp(logits - top[:, 0:1])
        run_sum[...] = run_sum[...] * scale + jnp.sum(weights, axis=1, keepdims=True)
        run_acc[...] = run_acc[...] * scale + dot(weights.astype(BF16), block[:, cols:])
        run_top[...] = top

    all_z(stats, 1, gr.at[1, 0]).wait_recv()
    all_y(stats, 1).start()
    q_send().wait_recv()
    queries[2 * seq : 3 * seq], queries[3 * seq :] = both_heads(q_pair[1 - y])
    kv_c(0).wait_recv()
    attend(0)
    all_y(stats, 1).wait_recv()
    all_c(stats, 1).start()
    all_c(stats, 1).wait_recv()

    st = stats[...].reshape(rows, LANES)
    at = lane(rows)

    def group(lo):
        kept = jnp.where((at >= lo) & (at < lo + 32), st, 0.0)
        kept = kept + pltpu.roll(kept, 64, 1)
        return kept + pltpu.roll(kept, 32, 1)

    tops[...] = group(0)
    invs[...] = 1.0 / group(32)
    inners[...] = group(64)

    def x_send(s, d):
        return send(gterm.at[s, lax.rem(x + d, NX)], x_in.at[s, d], rs.at[0], rr.at[0, s], at_x(d))

    def all_x(s):
        return send(gterm.at[s, pl.ds(0, NX - 1)], x_in.at[s, pl.ds(1, NX - 1)], rs.at[0], rr.at[0, s], at_x(1))

    def backward(s):
        def part_of(i, carry):
            at = pl.ds(pl.multiple_of(i * half, half), half)
            ge = grads[pl.ds(i * (NZ // 2), NZ // 2)].reshape(half, width)
            probs = jnp.exp(scores[s, at, :] - tops[at, :]) * invs[at, :]
            ds = probs * (slot_inner[s, at, :] - inners[at, :])
            ds = jnp.where(lane(half) < heads, ds, 0.0).astype(BF16)
            dvalue[...] = (wide(probs, width) * ge).astype(BF16)
            dembed[at, :] = (dot_nt(dvalue[...], wvp[...]) + dot_nt(ds, kq_rep[...])).astype(BF16)
            return carry

        lax.fori_loop(0, 2, part_of, 0)
        wx = width // NX
        for i in range(NX):
            term = dot(patches[s], dembed[:, i * wx : (i + 1) * wx])
            gterm[s, i] = term
        for d in range(1, NX):
            x_send(s, d).start()

    def slot_step(s, carry):
        backward(s)
        kv_pass(2 * s + 1)

        @pl.when(s < slots - 1)
        def _():
            kv_pass(2 * s + 2)

        return carry

    lax.fori_loop(0, slots, slot_step, 0)

    def key_step(k, carry):
        kv_c(k).wait_recv()
        attend(k)
        return carry

    lax.fori_loop(1, NZ, key_step, 0)

    acc_out[...] = jnp.where(left, run_acc[2 * seq : 3 * seq], run_acc[3 * seq :])
    at = lane(seq)
    table = jnp.where(at == 0, run_top[2 * seq : 3 * seq], run_top[3 * seq :])
    table = jnp.where(at == 2, run_sum[2 * seq : 3 * seq], jnp.where(at == 3, run_sum[3 * seq :], table))
    ml_out[...] = table.T[0:8]
    back_send(acc_out, acc_in, 1).start()
    back_send(ml_out, ml_in, 2).start()

    def l_send(s):
        return send(l_out.at[s], l_in.at[s], rs.at[1], rr.at[1, s], l_mate)

    near_col = pl.multiple_of(w * cols, cols)
    other = pl.multiple_of((1 - w) * cols, cols)

    def x_sum(s, carry):
        all_x(s).wait_recv()

        def summed(at):
            terms = [x_in[s, d, :, pl.ds(at, cols)] for d in range(1, NX)]
            return gterm[s, x, :, pl.ds(at, cols)] + (terms[0] + terms[1] + terms[2])

        l_out[s] = summed(other)
        l_send(s).start()
        embed_grad[s] = summed(near_col)
        return carry

    lax.fori_loop(0, slots, x_sum, 0)

    back_send(acc_out, acc_in, 1).wait_recv()
    back_send(ml_out, ml_in, 2).wait_recv()
    table = jnp.concatenate([ml_in[...], jnp.zeros((seq - 8, seq), F32)], axis=0).T
    m1 = jnp.where(left, run_top[0:seq], run_top[seq : 2 * seq])
    l1 = jnp.where(left, run_sum[0:seq], run_sum[seq : 2 * seq])
    a1 = jnp.where(left, run_acc[0:seq], run_acc[seq : 2 * seq])
    m2 = jnp.where(left, table[:, 0:1], table[:, 1:2])
    l2 = jnp.where(left, table[:, 2:3], table[:, 3:4])
    top = jnp.maximum(m1, m2)
    e1, e2 = jnp.exp(m1 - top), jnp.exp(m2 - top)
    mixed = (a1 * e1 + acc_in[...] * e2) / (l1 * e1 + l2 * e2)
    kept = tokens[:, :, pl.ds(pl.multiple_of(j * cols, cols), cols)].reshape(seq, cols)
    layer_out[...] = kept.astype(F32) + mixed

    def l_sum(s, carry):
        l_send(s).wait_recv()
        embed_grad[s] = embed_grad[s] + l_in[s]
        return carry

    lax.fori_loop(0, slots, l_sum, 0)

    send(part.at[pl.ds(0, NZ), pl.ds(0, NY), 1 - c], sib_in, bs.at[0], br.at[0, 0], c_mate).wait_send()
    send(y_out, y_in, bs.at[1], br.at[1, 0], y_mate).wait_send()
    all_b_far().wait_send()
    all_b_z().wait_send()
    all_z(stats, 1, gr.at[1, 0]).wait_send()
    all_y(stats, 1).wait_send()
    all_c(stats, 1).wait_send()
    grad_y().wait_send()
    grads_left = grads.at[pl.ds(0, NZ - 1), pl.ds(0, NY), c]
    send(grads_left, grads_left, gs.at[0, 0], er.at[2, 0], at_z(1)).wait_send()
    all_grad_c().wait_send()
    kv_left = kv.at[pl.ds(0, NZ - 1), c]
    send(kv_left, kv_left, gs.at[2, 0], er.at[0, 0], at_z(1)).wait_send()
    kv_left = kv.at[pl.ds(0, NZ), c]
    send(kv_left, kv_left, gs.at[2, 1], er.at[1, 0], c_mate).wait_send()
    q_send().wait_send()
    back_send(acc_out, acc_in, 1).wait_send()
    back_send(ml_out, ml_in, 2).wait_send()
    all_tok().wait_send()
    x_left = gterm.at[pl.ds(0, slots), pl.ds(0, NX - 1)]
    send(x_left, x_left, rs.at[0], rr.at[0, 0], at_x(1)).wait_send()
    send(l_out, l_in, rs.at[1], rr.at[1, 0], l_mate).wait_send()


def per_device(
    patches,
    slot_weight,
    slot_bias,
    var_embed,
    owner_count,
    slot_variable,
    key_query,
    value_weight,
    norm_gain,
    qkv_weight,
    token_grad,
):
    slots, pixels, rows = patches.shape
    width = value_weight.shape[0]
    piece = token_grad.shape[0]
    cols = qkv_weight.shape[2]
    seq = NX * NL * piece
    zy = (NZ, NY, NC)
    mw = width + LANES
    dma = pltpu.SemaphoreType.DMA
    vm = pltpu.VMEM
    scratch = [
        vm((slots, pixels, rows), BF16),
        vm((slots, pixels, width), BF16),
        vm(var_embed.shape, F32),
        vm((width, width), BF16),
        vm((3, width, cols), BF16),
        vm((width, width), BF16),
        vm((width, width), BF16),
        vm((width, LANES), BF16),
        vm((slots, rows, width), BF16),
        vm((slots, rows, width), F32),
        vm((slots, rows, LANES), F32),
        vm((slots, rows, LANES), F32),
        vm((NZ, NY, NC, piece, mw), F32),
        vm((NZ, NY, piece, mw), F32),
        vm((NZ, piece, mw), F32),
        vm((NZ, piece, mw), F32),
        vm((NZ, piece, mw), F32),
        vm((NZ, piece, mw), F32),
        vm((NZ, piece, mw), F32),
        vm((FAR, piece, mw), BF16),
        vm((FAR, piece, mw), BF16),
        vm(zy + (piece, width), F32),
        vm((slots, rows, LANES), F32),
        vm(zy + (piece, LANES), F32),
        vm((rows, LANES), F32),
        vm((rows, LANES), F32),
        vm((rows, LANES), F32),
        vm((NX * NL, piece, width), BF16),
        vm((4 * seq, cols), BF16),
        vm((NY, seq, cols), BF16),
        vm((NZ, NC, seq, 2 * cols), BF16),
        vm((seq, cols), F32),
        vm((seq, cols), F32),
        vm((8, seq), F32),
        vm((8, seq), F32),
        vm((4 * seq, LANES), F32),
        vm((4 * seq, LANES), F32),
        vm((4 * seq, cols), F32),
        vm((rows // 2, width), BF16),
        vm((rows, width), BF16),
        vm((slots, NX, pixels, width // NX), F32),
        vm((slots, NX, pixels, width // NX), F32),
        vm((slots, pixels, cols), F32),
        vm((slots, pixels, cols), F32),
        dma((4,)),
        dma((3, NZ)),
        dma((3, 3)),
        dma((2, 5)),
        dma((3, NZ)),
        dma((1,)),
        dma((1,)),
        dma((2,)),
        dma((2, slots)),
        dma((5,)),
        dma((3,)),
        dma((3,)),
    ]
    in_vm = pl.BlockSpec(memory_space=pltpu.VMEM)
    in_hbm = pl.BlockSpec(memory_space=pl.ANY)
    in_sm = pl.BlockSpec(memory_space=pltpu.SMEM)
    return pl.pallas_call(
        kernel,
        out_shape=(
            jax.ShapeDtypeStruct((seq, cols), F32),
            jax.ShapeDtypeStruct((slots, pixels, cols), F32),
        ),
        in_specs=[in_hbm, in_hbm, in_vm, in_hbm, in_sm, in_sm, in_vm, in_hbm, in_vm, in_hbm, in_vm],
        out_specs=(in_vm, in_vm),
        scratch_shapes=scratch,
        compiler_params=pltpu.CompilerParams(
            collective_id=0, has_side_effects=True, vmem_limit_bytes=60 * 2**20
        ),
        name="sublayer",
    )(
        patches,
        slot_weight,
        slot_bias,
        var_embed,
        owner_count,
        slot_variable,
        key_query.T,
        value_weight,
        norm_gain.reshape(1, width),
        qkv_weight.transpose(1, 0, 2),
        token_grad,
    )


def solution(mesh):
    in_specs = (
        P("var", None, "tp"),
        P("var", None, None),
        P("var", None),
        P(),
        P("var"),
        P("var"),
        P(),
        P(),
        P(),
        P(None, None, "tp"),
        P(("var", "tp"), None),
    )
    out_specs = (P("var", "tp"), P("var", None, "tp"))
    return jax.shard_map(
        per_device, mesh=mesh, in_specs=in_specs, out_specs=out_specs, check_vma=False
    )
```

```python
import functools

import jax
import jax.numpy as jnp
from jax import lax
from jax.experimental import pallas as pl
from jax.experimental.pallas import tpu as pltpu
from jax.sharding import PartitionSpec as P

F32 = jnp.float32
BF16 = jnp.bfloat16
MESH = pl.DeviceIdType.MESH
LANES = 128
NEG = float("-inf")
NZ, NY, NC = 8, 2, 2
NX, NL = 4, 2
HOPS = (2, 5, 8, 11)
FAR = 4


def iota(shape, axis):
    return lax.broadcasted_iota(jnp.int32, shape, axis)


def near(k):
    return jnp.where(lax.rem(k, 2) == 1, (k + 1) // 2, lax.rem(NZ - k // 2, NZ))


def far(k):
    return jnp.where(lax.rem(k, 2) == 0, NZ // 2 + k // 2, NZ // 2 - 1 - k // 2)


def dot(a, b):
    return jnp.dot(a, b, preferred_element_type=F32)


def dot_nt(a, b):
    return lax.dot_general(a, b, (((1,), (1,)), ((), ())), preferred_element_type=F32)


def dot_tn(a, b):
    return lax.dot_general(a, b, (((0,), (0,)), ((), ())), preferred_element_type=F32)


def lane(rows):
    return iota((rows, LANES), 1)


def unpack_two(x):
    left = lane(x.shape[0]) < 64
    turned = pltpu.roll(x, 64, 1)
    return jnp.where(left, x, turned), jnp.where(left, turned, x)


def head_total(x):
    total = x[:, 0:LANES]
    for i in range(1, x.shape[1] // LANES):
        total = total + x[:, i * LANES : (i + 1) * LANES]
    for shift in (64, 32, 16):
        total = total + pltpu.roll(total, shift, 1)
    return total


def wide(x, width):
    return jnp.concatenate([x] * (width // LANES), axis=1)


def packed_two(top, total):
    return jnp.where(lane(top.shape[0]) < 64, top, total)


def thirds(x):
    a = x.astype(BF16).astype(F32)
    b = (x - a).astype(BF16).astype(F32)
    return a, b, x - a - b


def packed_six(top, total):
    at = lane(top.shape[0]) // 16
    t1, t2, t3 = thirds(top)
    l1, l2, l3 = thirds(total)
    out = jnp.where(at == 0, t2, jnp.where(at == 1, t1, jnp.where(at == 2, t3, 0.0)))
    return jnp.where(at == 4, l2, jnp.where(at == 5, l1, jnp.where(at == 6, l3, out))).astype(BF16)


def unpack_six(x):
    x = x.astype(F32)
    left = lane(x.shape[0]) < 64

    def whole(kept):
        for shift in (64, 32, 16):
            kept = kept + pltpu.roll(kept, shift, 1)
        return kept

    return whole(jnp.where(left, x, 0.0)), whole(jnp.where(left, 0.0, x))


def merged(first, second):
    s1, m1, l1 = first
    s2, m2, l2 = second
    width = s1.shape[1]
    top = jnp.maximum(m1, m2)
    e1, e2 = jnp.exp(m1 - top), jnp.exp(m2 - top)
    return s1 * wide(e1, width) + s2 * wide(e2, width), top, l1 * e1 + l2 * e2


def kernel(
    patches_hbm,
    slot_weight_hbm,
    slot_bias,
    var_embed_hbm,
    owner_count,
    slot_variable,
    key_query,
    value_weight_hbm,
    norm_gain,
    qkv_weight_hbm,
    token_grad,
    layer_out,
    embed_grad,
    patches,
    slot_weight,
    var_embed,
    value_weight,
    qkv_weight,
    perm,
    wvp,
    kq_rep,
    emb,
    values,
    scores,
    raw,
    part,
    sib_in,
    own,
    y_out,
    y_in,
    z_out,
    z_in,
    far_out,
    far_in,
    grads,
    slot_inner,
    stats,
    tops,
    invs,
    inners,
    tokens,
    queries,
    q_pair,
    kv,
    acc_out,
    acc_in,
    ml_out,
    ml_in,
    run_top,
    run_sum,
    run_acc,
    dvalue,
    dembed,
    gterm,
    x_in,
    l_out,
    l_in,
    bs,
    br,
    gs,
    gr,
    er,
    ts,
    tr,
    rs,
    rr,
    ls,
    ps,
    pr,
):
    slots, pixels, rows = patches.shape
    width = value_weight.shape[0]
    heads = key_query.shape[0]
    piece = token_grad.shape[0]
    head_dim = width // heads
    seq = tokens.shape[0] * piece
    cols = layer_out.shape[1]
    zrows = rows // NZ

    v, j = lax.axis_index("var"), lax.axis_index("tp")
    z, y, c = v // 4, lax.rem(v // 2, 2), lax.rem(v, 2)
    x, w = j // 2, lax.rem(j, 2)

    def at_z(dz):
        return {"var": lax.rem(z + dz, NZ) * 4 + y * 2 + c, "tp": j}

    y_mate = {"var": z * 4 + (1 - y) * 2 + c, "tp": j}
    c_mate = {"var": z * 4 + y * 2 + (1 - c), "tp": j}
    l_mate = {"var": v, "tp": x * 2 + (1 - w)}

    def at_tp(d):
        return {"var": v, "tp": lax.rem(j + d, NX * NL)}

    def at_x(d):
        return {"var": v, "tp": lax.rem(x + d, NX) * 2 + w}

    def send(src, dst, ssem, rsem, device):
        return pltpu.make_async_remote_copy(
            src_ref=src, dst_ref=dst, send_sem=ssem, recv_sem=rsem, device_id=device, device_id_type=MESH
        )

    barrier = pltpu.get_barrier_semaphore()

    def greet_z(d, carry):
        pl.semaphore_signal(barrier, inc=1, device_id=at_z(d), device_id_type=MESH)
        return carry

    def greet_tp(d, carry):
        pl.semaphore_signal(barrier, inc=1, device_id=at_tp(d), device_id_type=MESH)
        return carry

    lax.fori_loop(1, NZ, greet_z, 0)
    lax.fori_loop(1, NX * NL, greet_tp, 0)
    pl.semaphore_signal(barrier, inc=1, device_id=y_mate, device_id_type=MESH)
    pl.semaphore_signal(barrier, inc=1, device_id=c_mate, device_id_type=MESH)

    pairs = (
        (value_weight_hbm, value_weight),
        (patches_hbm, patches),
        (slot_weight_hbm, slot_weight),
        (var_embed_hbm, var_embed),
        (qkv_weight_hbm, qkv_weight),
    )
    loads = [pltpu.make_async_copy(src, dst, ls.at[i]) for i, (src, dst) in enumerate(pairs)]
    for load in loads:
        load.start()

    def g_start(buf, n, rsem):
        mine = buf.at[z, y, c]

        def one(k, carry):
            send(mine, mine, gs.at[n, 0], rsem(k), at_z(near(k))).start()
            return carry

        lax.fori_loop(1, NZ, one, 0)

    def all_z(buf, n, rsem):
        here = buf.at[pl.ds(0, NZ - 1), y, c]
        return send(here, here, gs.at[n, 0], rsem, at_z(1))

    def all_y(buf, n):
        here = buf.at[pl.ds(0, NZ), y, c]
        return send(here, here, gs.at[n, 1], gr.at[n, 1], y_mate)

    def all_c(buf, n):
        here = buf.at[pl.ds(0, NZ), pl.ds(0, NY), c]
        return send(here, here, gs.at[n, 2], gr.at[n, 2], c_mate)

    def z_of(k):
        return lax.rem(z - near(k) + NZ, NZ)

    def kv_z(k):
        here = kv.at[z_of(k), c]
        return send(here, here, gs.at[2, 0], er.at[0, k], at_z(near(k)))

    def kv_c(k):
        here = kv.at[z_of(k), c]
        return send(here, here, gs.at[2, 1], er.at[1, k], c_mate)

    def kv_pass(k):
        kv_z(k).wait_recv()
        kv_c(k).start()

    def q_send():
        return send(q_pair.at[y], q_pair.at[y], ps.at[0], pr.at[0], y_mate)

    def back_send(src, dst, n):
        return send(src, dst, ps.at[n], pr.at[n], y_mate)

    def grad_y():
        here = grads.at[z, y, c]
        return send(here, here, gs.at[0, 1], gr.at[0, 1], y_mate)

    def grad_z(k, to, dz):
        here = grads.at[z_of(k), pl.ds(0, NY), c]
        return send(here, here, gs.at[0, 0], er.at[2, to], at_z(dz))

    def grad_c(k):
        here = grads.at[z_of(k), pl.ds(0, NY), c]
        return send(here, here, gs.at[0, 2], gr.at[0, 2], c_mate)

    def grad_pass(k):
        grad_z(k, k, 1).wait_recv()
        if k <= NZ - 3:
            grad_z(k, k + 2, 1 if k % 2 else NZ - 1).start()
        grad_c(k).start()

    def grad_first():
        grad_y().wait_recv()
        grad_z(0, 1, 1).start()
        grad_z(0, 2, NZ - 1).start()
        grad_c(0).start()

    def all_grad_c():
        here = grads.at[pl.ds(0, NZ), pl.ds(0, NY), c]
        return send(here, here, gs.at[0, 2], gr.at[0, 2], c_mate)

    def grad_hop(n):
        for k in (2 * n + 1, 2 * n + 2):
            if k < NZ:
                grad_pass(k)

    loads[0].wait()

    def make_perm(i, carry):
        cb = pl.multiple_of(i * 256, 256)
        row, col = iota((width, 256), 0), iota((width, 256), 1) + cb
        hit = lax.rem(row, head_dim) * heads + row // head_dim == col
        block = jnp.where(hit, 1.0, 0.0).astype(BF16)
        perm[:, pl.ds(cb, 256)] = block
        wvp[:, pl.ds(cb, 256)] = dot(value_weight[...], block).astype(BF16)
        return carry

    lax.fori_loop(0, width // 256, make_perm, 0)

    g1, g2, g3 = thirds(token_grad[...])
    gp = dot(jnp.concatenate([g1, g2, g3], axis=0).astype(BF16), perm[...])
    gp = gp[0:piece] + (gp[piece : 2 * piece] + gp[2 * piece :])
    grads[z, y, c] = gp

    pl.semaphore_wait(barrier, NZ - 1 + NX * NL - 1 + 2)
    grad_y().start()

    spread = jnp.where(lax.rem(iota((heads, LANES), 1), heads) == iota((heads, LANES), 0), 1.0, 0.0).astype(BF16)
    kq_rep[...] = dot_tn(key_query[...], spread).astype(BF16)

    for load in loads[1:4]:
        load.wait()
    for s in range(slots):
        offset = slot_bias[s : s + 1, :] + var_embed[pl.ds(slot_variable[s], 1), :]
        emb[s] = (dot_tn(patches[s], slot_weight[s]) + offset).astype(BF16)
        bias = jnp.where(s < owner_count[0], 0.0, NEG)
        scores[s] = dot(emb[s], kq_rep[...]) + bias
    top = scores[0]
    for s in range(1, slots):
        top = jnp.maximum(top, scores[s])
    total = jnp.zeros_like(top)
    for s in range(slots):
        e = jnp.exp(scores[s] - top)
        raw[s] = e
        total = total + e
    tops[...] = top
    invs[...] = total
    grad_first()

    def b_c(k):
        return send(part.at[k, pl.ds(0, NY), 1 - c], sib_in.at[k], bs.at[0], br.at[0, k], c_mate)

    def b_y(k):
        return send(y_out.at[k], y_in.at[k], bs.at[1], br.at[1, k], y_mate)

    def b_z(k):
        return send(z_out.at[k], z_in.at[k], bs.at[2], br.at[2, 0], at_z(far(k)))

    def b_far(k):
        return send(far_out.at[k], far_in.at[k], bs.at[3], br.at[2, 1], at_z(far(k)))

    def all_b_z():
        at = pl.ds(FAR, NZ - 1 - FAR)
        return send(z_out.at[at], z_in.at[at], bs.at[2], br.at[2, 0], at_z(1))

    def all_b_far():
        return send(far_out, far_in, bs.at[3], br.at[2, 1], at_z(1))

    def first_stage(k):
        start = pl.multiple_of(lax.rem(z + far(k), NZ) * zrows, zrows)
        e = emb[:, pl.ds(start, zrows), :].reshape(slots * zrows, width)
        val = dot(e, wvp[...]).reshape(slots, zrows, width)
        values[:, pl.ds(start, zrows), :] = val
        for i in range(width // LANES):
            at = slice(i * LANES, (i + 1) * LANES)
            acc = raw[0, pl.ds(start, zrows), :] * val[0, :, at]
            for s in range(1, slots):
                acc = acc + raw[s, pl.ds(start, zrows), :] * val[s, :, at]
            part[k, :, :, :, at] = acc.reshape(NY, NC, piece, LANES)
        both = packed_two(tops[pl.ds(start, zrows), :], invs[pl.ds(start, zrows), :])
        part[k, :, :, :, width:] = both.reshape(NY, NC, piece, LANES)
        b_c(k).start()

    def both_of(ref):
        return (ref[:, 0:width], *unpack_two(ref[:, width:]))

    def six_of(ref):
        return (ref[:, 0:width].astype(F32), *unpack_six(ref[:, width:]))

    def second_stage(k):
        b_c(k).wait_recv()
        sums, m, l = merged(both_of(part.at[k, 1 - y, c]), both_of(sib_in.at[k, 1 - y]))
        y_out[k, :, 0:width] = sums
        y_out[k, :, width:] = packed_two(m, l)
        b_y(k).start()
        sums, m, l = merged(both_of(part.at[k, y, c]), both_of(sib_in.at[k, y]))
        own[k, :, 0:width] = sums
        own[k, :, width:] = packed_two(m, l)

    def third_stage(k):
        b_y(k).wait_recv()
        sums, m, l = merged(both_of(own.at[k]), both_of(y_in.at[k]))

        @pl.when(k < FAR)
        def _():
            far_out[k, :, 0:width] = sums.astype(BF16)
            far_out[k, :, width:] = packed_six(m, l)
            b_far(k).start()

        @pl.when((k >= FAR) & (k < NZ - 1))
        def _():
            z_out[k, :, 0:width] = sums
            z_out[k, :, width:] = packed_two(m, l)
            b_z(k).start()

        @pl.when(k == NZ - 1)
        def _():
            own[k, :, 0:width] = sums
            own[k, :, width:] = packed_two(m, l)

    def step(i, carry):
        @pl.when(i < NZ)
        def _():
            first_stage(i)

        @pl.when((i >= 2) & (i < NZ + 2))
        def _():
            second_stage(i - 2)

        @pl.when(i >= 4)
        def _():
            third_stage(i - 4)

        for n in range(NZ // 2):
            pl.when(i == HOPS[n])(functools.partial(grad_hop, n))
        return carry

    lax.fori_loop(0, NZ + 4, step, 0)

    all_b_far().wait_recv()
    all_b_z().wait_recv()
    terms = [both_of(own.at[NZ - 1])] + [six_of(far_in.at[k]) for k in range(FAR)]
    terms += [both_of(z_in.at[k]) for k in range(FAR, NZ - 1)]
    top = functools.reduce(jnp.maximum, [m for _, m, _ in terms])
    es = [jnp.exp(m - top) for _, m, _ in terms]
    total = functools.reduce(jnp.add, [l * e for (_, _, l), e in zip(terms, es)])
    sums = functools.reduce(jnp.add, [t * wide(e, width) for (t, _, _), e in zip(terms, es)])
    agg = (sums / wide(total, width)).astype(BF16)
    tokens[j] = dot_nt(agg, perm[...]).astype(BF16)

    def tok(d):
        return send(tokens.at[j], tokens.at[j], ts.at[0], tr.at[0], at_tp(d))

    def all_tok():
        here = tokens.at[pl.ds(0, NX * NL - 1)]
        return send(here, here, ts.at[0], tr.at[0], at_tp(1))

    def tok_start(d, carry):
        tok(d).start()
        return carry

    lax.fori_loop(1, NX * NL, tok_start, 0)

    inner = head_total(gp * agg.astype(F32))
    at = lane(piece)
    stats[z, y, c] = jnp.where(at < 32, top, jnp.where(at < 64, total, inner))
    g_start(stats, 1, lambda k: gr.at[1, 0])

    half = rows // 2

    def inner_of(h):
        at = slice(h * half, (h + 1) * half)

        def one(s, carry):
            ge = grads[h * (NZ // 2) : (h + 1) * (NZ // 2)].reshape(half, width)
            slot_inner[s, at, :] = head_total(values[s, at, :] * ge)
            return carry

        lax.fori_loop(0, slots, one, 0)

    all_tok().wait_recv()
    loads[4].wait()

    tf = tokens[...].reshape(seq, width).astype(F32)
    centred = tf - jnp.mean(tf, axis=1, keepdims=True)
    spread_sq = jnp.mean(centred * centred, axis=1, keepdims=True)
    normed = (centred * lax.rsqrt(spread_sq + 1e-05) * norm_gain[...]).astype(BF16)
    all_qkv = jnp.concatenate([qkv_weight[i] for i in range(3)], axis=1)
    projected = dot(normed, all_qkv).astype(BF16)
    mine = kv.at[z, c]
    mine[...] = projected[:, cols:]

    def kv_start(k, carry):
        send(mine, mine, gs.at[2, 0], er.at[0, k], at_z(near(k))).start()
        return carry

    lax.fori_loop(1, NZ, kv_start, 0)
    q_pair[y] = projected[:, 0:cols]
    q_send().start()
    kv_c(0).start()
    left = iota((seq, cols), 1) < head_dim

    def both_heads(q):
        q = q.astype(F32) * (head_dim ** (-0.5))
        return jnp.where(left, q, 0.0).astype(BF16), jnp.where(left, 0.0, q).astype(BF16)

    queries[0:seq], queries[seq : 2 * seq] = both_heads(projected[:, 0:cols])
    run_top[...] = jnp.full_like(run_top, NEG)
    run_sum[...] = jnp.zeros_like(run_sum)
    run_acc[...] = jnp.zeros_like(run_acc)
    def attend(k):
        block = kv[z_of(k)].reshape(NC * seq, 2 * cols)
        logits = dot_nt(queries[...], block[:, 0:cols])
        top = jnp.maximum(run_top[...], jnp.max(logits, axis=1, keepdims=True))
        scale = jnp.exp(run_top[...] - top)
        weights = jnp.exp(logits - top[:, 0:1])
        run_sum[...] = run_sum[...] * scale + jnp.sum(weights, axis=1, keepdims=True)
        run_acc[...] = run_acc[...] * scale + dot(weights.astype(BF16), block[:, cols:])
        run_top[...] = top

    all_z(stats, 1, gr.at[1, 0]).wait_recv()
    all_y(stats, 1).start()
    q_send().wait_recv()
    queries[2 * seq : 3 * seq], queries[3 * seq :] = both_heads(q_pair[1 - y])
    kv_c(0).wait_recv()
    attend(0)
    all_y(stats, 1).wait_recv()
    all_c(stats, 1).start()
    all_grad_c().wait_recv()
    inner_of(0)
    inner_of(1)
    all_c(stats, 1).wait_recv()

    st = stats[...].reshape(rows, LANES)
    at = lane(rows)

    def group(lo):
        kept = jnp.where((at >= lo) & (at < lo + 32), st, 0.0)
        kept = kept + pltpu.roll(kept, 64, 1)
        return kept + pltpu.roll(kept, 32, 1)

    tops[...] = group(0)
    invs[...] = 1.0 / group(32)
    inners[...] = group(64)

    def x_send(s, d):
        return send(gterm.at[s, lax.rem(x + d, NX)], x_in.at[s, d], rs.at[0], rr.at[0, s], at_x(d))

    def all_x(s):
        return send(gterm.at[s, pl.ds(0, NX - 1)], x_in.at[s, pl.ds(1, NX - 1)], rs.at[0], rr.at[0, s], at_x(1))

    def backward(s):
        def part_of(i, carry):
            at = pl.ds(pl.multiple_of(i * half, half), half)
            ge = grads[pl.ds(i * (NZ // 2), NZ // 2)].reshape(half, width)
            probs = jnp.exp(scores[s, at, :] - tops[at, :]) * invs[at, :]
            ds = probs * (slot_inner[s, at, :] - inners[at, :])
            ds = jnp.where(lane(half) < heads, ds, 0.0).astype(BF16)
            dvalue[...] = (wide(probs, width) * ge).astype(BF16)
            dembed[at, :] = (dot_nt(dvalue[...], wvp[...]) + dot_nt(ds, kq_rep[...])).astype(BF16)
            return carry

        lax.fori_loop(0, 2, part_of, 0)
        wx = width // NX
        for i in range(NX):
            term = dot(patches[s], dembed[:, i * wx : (i + 1) * wx])
            gterm[s, i] = term
        for d in range(1, NX):
            x_send(s, d).start()

    def key_step(k, carry):
        kv_c(k).wait_recv()
        attend(k)
        return carry

    def slot_step(s, carry):
        backward(s)
        kv_pass(2 * s + 1)

        @pl.when(s < slots - 1)
        def _():
            kv_pass(2 * s + 2)

        @pl.when(s >= 2)
        def _():
            key_step(2 * s - 3, 0)
            key_step(2 * s - 2, 0)

        return carry

    lax.fori_loop(0, slots, slot_step, 0)

    lax.fori_loop(5, NZ, key_step, 0)

    acc_out[...] = jnp.where(left, run_acc[2 * seq : 3 * seq], run_acc[3 * seq :])
    at = lane(seq)
    table = jnp.where(at == 0, run_top[2 * seq : 3 * seq], run_top[3 * seq :])
    table = jnp.where(at == 2, run_sum[2 * seq : 3 * seq], jnp.where(at == 3, run_sum[3 * seq :], table))
    ml_out[...] = table.T[0:8]
    back_send(acc_out, acc_in, 1).start()
    back_send(ml_out, ml_in, 2).start()

    def l_send(s):
        return send(l_out.at[s], l_in.at[s], rs.at[1], rr.at[1, s], l_mate)

    near_col = pl.multiple_of(w * cols, cols)
    other = pl.multiple_of((1 - w) * cols, cols)

    def x_sum(s, carry):
        all_x(s).wait_recv()

        def summed(at):
            terms = [x_in[s, d, :, pl.ds(at, cols)] for d in range(1, NX)]
            return gterm[s, x, :, pl.ds(at, cols)] + (terms[0] + terms[1] + terms[2])

        l_out[s] = summed(other)
        l_send(s).start()
        embed_grad[s] = summed(near_col)
        return carry

    lax.fori_loop(0, slots, x_sum, 0)

    back_send(acc_out, acc_in, 1).wait_recv()
    back_send(ml_out, ml_in, 2).wait_recv()
    table = jnp.concatenate([ml_in[...], jnp.zeros((seq - 8, seq), F32)], axis=0).T
    m1 = jnp.where(left, run_top[0:seq], run_top[seq : 2 * seq])
    l1 = jnp.where(left, run_sum[0:seq], run_sum[seq : 2 * seq])
    a1 = jnp.where(left, run_acc[0:seq], run_acc[seq : 2 * seq])
    m2 = jnp.where(left, table[:, 0:1], table[:, 1:2])
    l2 = jnp.where(left, table[:, 2:3], table[:, 3:4])
    top = jnp.maximum(m1, m2)
    e1, e2 = jnp.exp(m1 - top), jnp.exp(m2 - top)
    mixed = (a1 * e1 + acc_in[...] * e2) / (l1 * e1 + l2 * e2)
    kept = tokens[:, :, pl.ds(pl.multiple_of(j * cols, cols), cols)].reshape(seq, cols)
    layer_out[...] = kept.astype(F32) + mixed

    def l_sum(s, carry):
        l_send(s).wait_recv()
        embed_grad[s] = embed_grad[s] + l_in[s]
        return carry

    lax.fori_loop(0, slots, l_sum, 0)

    send(part.at[pl.ds(0, NZ), pl.ds(0, NY), 1 - c], sib_in, bs.at[0], br.at[0, 0], c_mate).wait_send()
    send(y_out, y_in, bs.at[1], br.at[1, 0], y_mate).wait_send()
    all_b_far().wait_send()
    all_b_z().wait_send()
    all_z(stats, 1, gr.at[1, 0]).wait_send()
    all_y(stats, 1).wait_send()
    all_c(stats, 1).wait_send()
    grad_y().wait_send()
    grads_left = grads.at[pl.ds(0, NZ - 1), pl.ds(0, NY), c]
    send(grads_left, grads_left, gs.at[0, 0], er.at[2, 0], at_z(1)).wait_send()
    all_grad_c().wait_send()
    kv_left = kv.at[pl.ds(0, NZ - 1), c]
    send(kv_left, kv_left, gs.at[2, 0], er.at[0, 0], at_z(1)).wait_send()
    kv_left = kv.at[pl.ds(0, NZ), c]
    send(kv_left, kv_left, gs.at[2, 1], er.at[1, 0], c_mate).wait_send()
    q_send().wait_send()
    back_send(acc_out, acc_in, 1).wait_send()
    back_send(ml_out, ml_in, 2).wait_send()
    all_tok().wait_send()
    x_left = gterm.at[pl.ds(0, slots), pl.ds(0, NX - 1)]
    send(x_left, x_left, rs.at[0], rr.at[0, 0], at_x(1)).wait_send()
    send(l_out, l_in, rs.at[1], rr.at[1, 0], l_mate).wait_send()


def per_device(
    patches,
    slot_weight,
    slot_bias,
    var_embed,
    owner_count,
    slot_variable,
    key_query,
    value_weight,
    norm_gain,
    qkv_weight,
    token_grad,
):
    slots, pixels, rows = patches.shape
    width = value_weight.shape[0]
    piece = token_grad.shape[0]
    cols = qkv_weight.shape[2]
    seq = NX * NL * piece
    zy = (NZ, NY, NC)
    mw = width + LANES
    dma = pltpu.SemaphoreType.DMA
    vm = pltpu.VMEM
    scratch = [
        vm((slots, pixels, rows), BF16),
        vm((slots, pixels, width), BF16),
        vm(var_embed.shape, F32),
        vm((width, width), BF16),
        vm((3, width, cols), BF16),
        vm((width, width), BF16),
        vm((width, width), BF16),
        vm((width, LANES), BF16),
        vm((slots, rows, width), BF16),
        vm((slots, rows, width), F32),
        vm((slots, rows, LANES), F32),
        vm((slots, rows, LANES), F32),
        vm((NZ, NY, NC, piece, mw), F32),
        vm((NZ, NY, piece, mw), F32),
        vm((NZ, piece, mw), F32),
        vm((NZ, piece, mw), F32),
        vm((NZ, piece, mw), F32),
        vm((NZ, piece, mw), F32),
        vm((NZ, piece, mw), F32),
        vm((FAR, piece, mw), BF16),
        vm((FAR, piece, mw), BF16),
        vm(zy + (piece, width), F32),
        vm((slots, rows, LANES), F32),
        vm(zy + (piece, LANES), F32),
        vm((rows, LANES), F32),
        vm((rows, LANES), F32),
        vm((rows, LANES), F32),
        vm((NX * NL, piece, width), BF16),
        vm((4 * seq, cols), BF16),
        vm((NY, seq, cols), BF16),
        vm((NZ, NC, seq, 2 * cols), BF16),
        vm((seq, cols), F32),
        vm((seq, cols), F32),
        vm((8, seq), F32),
        vm((8, seq), F32),
        vm((4 * seq, LANES), F32),
        vm((4 * seq, LANES), F32),
        vm((4 * seq, cols), F32),
        vm((rows // 2, width), BF16),
        vm((rows, width), BF16),
        vm((slots, NX, pixels, width // NX), F32),
        vm((slots, NX, pixels, width // NX), F32),
        vm((slots, pixels, cols), F32),
        vm((slots, pixels, cols), F32),
        dma((4,)),
        dma((3, NZ)),
        dma((3, 3)),
        dma((2, 5)),
        dma((3, NZ)),
        dma((1,)),
        dma((1,)),
        dma((2,)),
        dma((2, slots)),
        dma((5,)),
        dma((3,)),
        dma((3,)),
    ]
    in_vm = pl.BlockSpec(memory_space=pltpu.VMEM)
    in_hbm = pl.BlockSpec(memory_space=pl.ANY)
    in_sm = pl.BlockSpec(memory_space=pltpu.SMEM)
    return pl.pallas_call(
        kernel,
        out_shape=(
            jax.ShapeDtypeStruct((seq, cols), F32),
            jax.ShapeDtypeStruct((slots, pixels, cols), F32),
        ),
        in_specs=[in_hbm, in_hbm, in_vm, in_hbm, in_sm, in_sm, in_vm, in_hbm, in_vm, in_hbm, in_vm],
        out_specs=(in_vm, in_vm),
        scratch_shapes=scratch,
        compiler_params=pltpu.CompilerParams(
            collective_id=0, has_side_effects=True, vmem_limit_bytes=60 * 2**20
        ),
        name="sublayer",
    )(
        patches,
        slot_weight,
        slot_bias,
        var_embed,
        owner_count,
        slot_variable,
        key_query.T,
        value_weight,
        norm_gain.reshape(1, width),
        qkv_weight.transpose(1, 0, 2),
        token_grad,
    )


def solution(mesh):
    in_specs = (
        P("var", None, "tp"),
        P("var", None, None),
        P("var", None),
        P(),
        P("var"),
        P("var"),
        P(),
        P(),
        P(),
        P(None, None, "tp"),
        P(("var", "tp"), None),
    )
    out_specs = (P("var", "tp"), P("var", None, "tp"))
    return jax.shard_map(
        per_device, mesh=mesh, in_specs=in_specs, out_specs=out_specs, check_vma=False
    )
```
